32 devices in a mesh: groups: 2 (over y), lat: 4 (over x, core), lon: 4 (over z).
Axes of the slice: x: 2, y: 2, z: 4, core: 2. Of those that a mesh axis runs over, the one named last changes fastest.
Arguments:
- tracers: float32 [256, 256, 128], P(('groups', 'lat'), 'lon'), parts along dimension 0, may hold values from 0.3 to 12.6, as said below
- shifts: float32 [4, 3, 16, 32], P('groups'), parts along dimension 0, may hold values from 0 to 1
- diffusivity: float32 [128], P('lat'), may hold values from 0.02 to 0.2, as said below
- source_patch: int32 [4, 16, 32], P('groups'), parts along dimension 0, may hold values from 0 to 511, as said below
Outputs:
- advanced: float32 [256, 256, 128], P(('groups', 'lat'), 'lon'), parts along dimension 0
The draws below stay inside these ranges and needn't reach their ends.
There are 2 independent parts, one for each index of `groups`. The reference program is written for one: setup_inputs(seed, part) draws one part's arguments, and reference() takes and returns one part's arrays. A program takes and returns all parts, laid end to end along the dimension named above; an argument that names none is the same for every part. Nothing has to cross between parts.
Inputs may be any that keep to these rules, and one draw needn't show every extreme that they name: `source_patch`: entry [s, r, c] is the global index of the departure patch of destination patch (r, c) in step s; the departure patch lies in the same tile of 8 patch columns as the destination, and in the same band of 4 patch rows or in one of the two bands on either side. For each step, tile, destination band and other source band, at most 4 destination patches take their departure patch there, and every destination band has a source band that gives exactly 4. `tracers`: positive mixing ratios. `diffusivity`: positive diffusion numbers.
All inputs are finite; a program needn't handle non-finite values.
Results may differ from the reference program's by a relative error of at most 0.0003.
Values sent between devices are 32-bit elements; how exact they have to be, the bound alone decides.
A program may use at most 64 MiB of HBM per device.

```python
import math
import jax
import jax.numpy as jnp
from jax import lax

TR = 32
LEV = 4
STEPS = 2
CAP = 4
CLAT = 32
CLON = 64
NLAT = 128
NLON = 256
PLAT = 16
PLON = 32


def draw_tracers(key, part):
    key_list = jax.random.split(jax.random.fold_in(key, 11), 2)
    tracer_scale = jnp.exp(jax.random.uniform(key_list[0], (TR,), jnp.float32, math.log(0.61), math.log(2.78)))
    channel = jnp.tile(tracer_scale, LEV)
    level_sign = jnp.where(jnp.arange(LEV) % 2 == 0, 1.0, -1.0).astype(jnp.float32)
    value_sign = jnp.repeat(level_sign, TR)
    inner_place = (jnp.arange(NLAT) % 8).astype(jnp.float32) / 7.0
    profile = 1.0 + (inner_place[:, None] - 0.5) * value_sign[None, :]
    base_value = jax.random.uniform(key_list[1], (NLAT, NLON, LEV * TR), jnp.float32, 1.0, 3.0)
    return (base_value * profile[:, None, :] * channel[None, None, :]).astype(jnp.float32)


def draw_diffusivity(key, part):
    inner_place = jnp.arange(NLAT) % 8
    lower = jnp.where(inner_place == 0, 0.1, 0.02).astype(jnp.float32)
    upper = jnp.where(inner_place == 7, 0.05, 0.2).astype(jnp.float32)
    unit = jax.random.uniform(jax.random.fold_in(key, 37), (NLAT,), jnp.float32, 0.0, 1.0)
    result = jnp.exp(jnp.log(lower) + (jnp.log(upper) - jnp.log(lower)) * unit)
    return jnp.clip(result, 0.02, 0.2).astype(jnp.float32)


def draw_source_patch(key, part):
    key_list = jax.random.split(jax.random.fold_in(key, 23), 5)
    per_rows = CLAT // 8
    per_cols = CLON // 8
    per_device = per_rows * per_cols
    lat_devs = NLAT // CLAT
    lon_devs = NLON // CLON
    dest_dev = jnp.arange(lat_devs)[None, None, :]
    jet_rows = jax.random.randint(key_list[0], (STEPS, lon_devs, 1), 0, lat_devs)
    reach_bands = jax.random.randint(key_list[4], (STEPS, lon_devs, lat_devs), 1, 3)
    edge_side = jnp.where(dest_dev < lat_devs - 1, 1, -1)
    toward = jnp.where(jet_rows > dest_dev, 1, jnp.where(jet_rows < dest_dev, -1, edge_side))
    first_pick = dest_dev + toward * reach_bands
    second_pick = dest_dev + toward
    third_pick = dest_dev - toward
    first_inside = (first_pick >= 0) & (first_pick < lat_devs)
    second_inside = (second_pick >= 0) & (second_pick < lat_devs)
    forced = jnp.where(first_inside, first_pick, jnp.where(second_inside, second_pick, third_pick))
    sources = jnp.arange(lat_devs)
    distance = jnp.abs(sources[None, :] - jnp.arange(lat_devs)[:, None])
    is_near = (distance >= 1) & (distance <= 2)
    counts = jax.random.randint(key_list[1], (STEPS, lon_devs, lat_devs, lat_devs), CAP // 2, CAP + 1)
    counts = jnp.where(is_near[None, None], counts, 0)
    counts = jnp.where(sources[None, None, None, :] == forced[..., None], CAP, counts)
    end_marks = jnp.cumsum(counts, axis=-1)
    places = jnp.arange(per_device)
    source_dev = jnp.sum((end_marks[..., None, :] <= places[:, None]).astype(jnp.int32), axis=-1)
    remote_total = end_marks[..., -1:]
    own_band = jnp.arange(lat_devs)[None, None, :, None]
    source_dev = jnp.where(places[None, None, None, :] < remote_total, source_dev, own_band)
    scores = jax.random.randint(key_list[2], (STEPS, lon_devs, lat_devs, per_device), 0, 1048576) * per_device + places
    shuffle = jnp.argsort(scores, axis=-1, stable=True)
    source_dev = jnp.take_along_axis(source_dev, shuffle, axis=-1)
    local_index = jax.random.randint(key_list[3], (STEPS, lon_devs, lat_devs, per_device), 0, per_device)
    tile_index = jnp.arange(lon_devs)[None, :, None, None]
    source_row = source_dev * per_rows + local_index // per_cols
    source_col = tile_index * per_cols + local_index % per_cols
    global_index = source_row * (NLON // 8) + source_col
    global_index = global_index.reshape(STEPS, lon_devs, lat_devs, per_rows, per_cols).transpose(0, 2, 3, 1, 4)
    return global_index.reshape(STEPS, NLAT // 8, NLON // 8).astype(jnp.int32)


def setup_inputs(seed: int = 0, part: int = 0) -> dict:
    arg_keys = jax.random.split(jax.random.key(seed), 5)
    part_keys = jax.random.split(jax.random.fold_in(arg_keys[4], part), 5)
    tracers = draw_tracers(jax.random.fold_in(jax.random.fold_in(arg_keys[4], part), 71), part)
    shifts = jnp.clip(jax.random.uniform(part_keys[1], (STEPS, 3, PLAT, PLON), jnp.float32, 0.0, 1.0), 0.0, 1.0)
    diffusivity = draw_diffusivity(jax.random.fold_in(arg_keys[4], 71), part)
    source_patch = draw_source_patch(jax.random.fold_in(jax.random.fold_in(arg_keys[4], part), 71), part)
    return {"tracers": tracers, "shifts": shifts, "diffusivity": diffusivity, "source_patch": source_patch}


def cubic_weights(fraction):
    first_term = -fraction * (fraction - 1.0) * (fraction - 2.0) / 6.0
    second_term = (fraction + 1.0) * (fraction - 1.0) * (fraction - 2.0) / 2.0
    third_term = -(fraction + 1.0) * fraction * (fraction - 2.0) / 2.0
    fourth_term = (fraction + 1.0) * fraction * (fraction - 1.0) / 6.0
    return (first_term, second_term, third_term, fourth_term)


def cubic_matrix(fraction, extent):
    places = jnp.arange(extent)
    running = jnp.zeros(fraction.shape + (extent, extent), jnp.float32)
    for offset, weight in zip(range(-1, 3), cubic_weights(fraction)):
        target_col = jnp.clip(places + offset, 0, extent - 1)
        indicator = (target_col[:, None] == places[None, :]).astype(jnp.float32)
        running = running + weight[..., None, None] * indicator
    return running


def interpolate(patches, fraction_y, fraction_x, fraction_z):
    patch_count = patches.shape[0]
    value_count = patches.shape[2]
    weight_y = cubic_matrix(fraction_y, 8)
    weight_x = cubic_matrix(fraction_x, 8)
    plane_weights = jnp.einsum("nac,nbd->nabcd", weight_y, weight_x, precision=lax.Precision.HIGHEST).reshape(patch_count, 64, 64)
    flat_result = jnp.einsum("nij,njv->niv", plane_weights, patches, precision=lax.Precision.HIGHEST)
    stacked = flat_result.reshape(patch_count, 64, LEV, value_count // LEV)
    weight_z = cubic_matrix(fraction_z, LEV)
    levelled = jnp.einsum("nlm,nimt->nilt", weight_z, stacked, precision=lax.Precision.HIGHEST)
    return levelled.reshape(patch_count, 64, value_count)


def to_patches(state_field):
    band_rows = state_field.shape[0] // 8
    band_cols = state_field.shape[1] // 8
    return state_field.reshape(band_rows, 8, band_cols, 8, -1).transpose(0, 2, 1, 3, 4).reshape(band_rows * band_cols, 64, -1)


def from_patches(patches, band_rows, band_cols):
    return patches.reshape(band_rows, band_cols, 8, 8, -1).transpose(0, 2, 1, 3, 4).reshape(band_rows * 8, band_cols * 8, -1)


def column_area(first_row, row_count, total_rows):
    latitude = ((first_row + jnp.arange(row_count)).astype(jnp.float32) + 0.5) * (math.pi / total_rows) - 0.5 * math.pi
    return jnp.cos(latitude)


def column_mass(state_field, weights):
    return jnp.sum(weights[:, None, None] * state_field, axis=(0, 1))


def diffuse(advected, diffusivity):
    padded = jnp.pad(advected, ((1, 1), (0, 0), (0, 0)))
    laplace = padded[2:] + padded[:-2] + jnp.roll(advected, -1, axis=1) + jnp.roll(advected, 1, axis=1) - 4.0 * advected
    return advected + diffusivity[:, None, None] * laplace


def reference(tracers, shifts, diffusivity, source_patch):
    weights = column_area(0, NLAT, NLAT)
    target = column_mass(tracers, weights)
    state_field = tracers
    for step_index in range(STEPS):
        departed = to_patches(state_field)[source_patch[step_index].reshape(-1)]
        fractions = shifts[step_index].reshape(3, -1)
        finished = interpolate(departed, fractions[0], fractions[1], fractions[2])
        advected = from_patches(finished, NLAT // 8, NLON // 8)
        diffused = diffuse(advected, diffusivity)
        state_field = diffused * (target / column_mass(diffused, weights))[None, None, :]
    return state_field
```

```python
import functools
import math

import jax
import jax.numpy as jnp
from jax import lax
from jax.experimental import pallas as pl
from jax.experimental.pallas import tpu as pltpu
from jax.sharding import PartitionSpec as P

LEV = 4
STEPS = 2
CAP = 4
OFFSETS = (-2, -1, 1, 2)
SENT_FIRST = (0, 3, 1, 2)
MESH = pl.DeviceIdType.MESH


def column_area(first_row, row_count, total_rows):
    latitude = ((first_row + jnp.arange(row_count)).astype(jnp.float32) + 0.5) * (
        math.pi / total_rows
    ) - 0.5 * math.pi
    return jnp.cos(latitude)


def cubic_weights(s):
    return (
        -s * (s - 1.0) * (s - 2.0) * (1.0 / 6.0),
        (s + 1.0) * (s - 1.0) * (s - 2.0) * 0.5,
        -(s + 1.0) * s * (s - 2.0) * 0.5,
        (s + 1.0) * s * (s - 1.0) * (1.0 / 6.0),
    )


def place_weights(w, place, last):
    a, b, c, d = w
    return (
        jnp.where(place == 0, 0.0, a),
        b + jnp.where(place == 0, a, 0.0) + jnp.where(place == last, c + d, 0.0),
        jnp.where(place == last, 0.0, c + jnp.where(place == last - 1, d, 0.0)),
        jnp.where(place >= last - 1, 0.0, d),
    )


def interpolate(rows, fractions, ratio):
    values = rows[0].shape[1]
    step = values // LEV
    column = lax.broadcasted_iota(jnp.int32, (8, values), 0)
    level = lax.broadcasted_iota(jnp.int32, (8, values), 1) // step
    sy, sx, sz = (jnp.full((8, values), s, jnp.float32) for s in fractions)
    a, b, c, d = cubic_weights(sy)
    ab, cd = a + b, c + d
    bcd = b + cd
    x = rows
    if ratio is not None:
        x = [r * ratio for r in x]
    out = [ab * x[0] + c * x[1] + d * x[2]]
    for i in range(1, 6):
        out.append(a * x[i - 1] + b * x[i] + c * x[i + 1] + d * x[i + 2])
    out.append(a * x[5] + b * x[6] + cd * x[7])
    out.append(a * x[6] + bcd * x[7])
    wx = place_weights(cubic_weights(sx), column, 7)
    wz = place_weights(cubic_weights(sz), level, LEV - 1)
    done = []
    for v in out:
        v = (
            wx[0] * pltpu.roll(v, 1, 0)
            + wx[1] * v
            + wx[2] * pltpu.roll(v, 7, 0)
            + wx[3] * pltpu.roll(v, 6, 0)
        )
        v = (
            wz[0] * pltpu.roll(v, step, 1)
            + wz[1] * v
            + wz[2] * pltpu.roll(v, values - step, 1)
            + wz[3] * pltpu.roll(v, values - 2 * step, 1)
        )
        done.append(v)
    return done


def kernel(
    br, bc, lats, lons,
    ti, tf, tr, out,
    st, arr, ia, snd, adv, outbuf, side_out, side_in, ka_out, ka_in, mass_out, mass_in,
    load_sem, store_sem, psend, precv, hsend, hrecv, ksend, krecv, msend, mrecv,
):
    np_ = br * bc
    rows = br * 8
    peers = lats * lons
    values = tr.shape[-1]
    lat = lax.axis_index("lat")
    lon = lax.axis_index("lon")
    kappa0 = STEPS * 3 * np_
    area0 = kappa0 + rows
    w0 = area0 + rows
    send0, arrive0, local0, pick0 = 0, 4 * CAP, 8 * CAP, 8 * CAP + np_
    per_step = 8 * CAP + 2 * np_

    loads = [
        pltpu.make_async_copy(
            tr.at[:, :, c], st.at[0, pl.ds(c * br, br)], load_sem.at[c]
        )
        for c in range(bc)
    ]
    for copy in loads:
        copy.start()

    zero = jnp.zeros((8, values), jnp.float32)
    for s in range(STEPS):
        for c in range(bc):
            adv[s, c, 0] = zero
            adv[s, c, rows + 1] = zero
    ka_in[...] = jnp.zeros_like(ka_in)
    ka_out[0] = jnp.full((1, values), tf[kappa0] * tf[area0], jnp.float32)
    ka_out[1] = jnp.full(
        (1, values), tf[kappa0 + rows - 1] * tf[area0 + rows - 1], jnp.float32
    )

    def peer(k):
        return {
            "lat": lax.rem(lat + k // lons, lats),
            "lon": lax.rem(lon + lax.rem(k, lons), lons),
        }

    barrier = pltpu.get_barrier_semaphore()

    def greet(k, _):
        pl.semaphore_signal(barrier, inc=1, device_id=peer(k), device_id_type=MESH)
        return 0

    lax.fori_loop(1, peers, greet, 0)
    pl.semaphore_wait(barrier, peers - 1)

    def in_range(offset):
        return (lat + offset >= 0) & (lat + offset < lats)

    def patch_copy(s, o):
        return pltpu.make_async_remote_copy(
            src_ref=snd.at[s, o],
            dst_ref=arr.at[s, 3 - o],
            send_sem=psend.at[s, o],
            recv_sem=precv.at[s, 3 - o],
            device_id={"lat": jnp.clip(lat + OFFSETS[o], 0, lats - 1), "lon": lon},
            device_id_type=MESH,
        )

    def ka_copy(i):
        return pltpu.make_async_remote_copy(
            src_ref=ka_out.at[i],
            dst_ref=ka_in.at[1 - i],
            send_sem=ksend.at[i],
            recv_sem=krecv.at[1 - i],
            device_id={"lat": jnp.clip(lat + 2 * i - 1, 0, lats - 1), "lon": lon},
            device_id_type=MESH,
        )

    def row_copy(s, i):
        return pltpu.make_async_remote_copy(
            src_ref=adv.at[s, :, rows if i else 1],
            dst_ref=adv.at[s, :, 0 if i else rows + 1],
            send_sem=hsend.at[s, i],
            recv_sem=hrecv.at[s, 1 - i],
            device_id={"lat": jnp.clip(lat + 2 * i - 1, 0, lats - 1), "lon": lon},
            device_id_type=MESH,
        )

    def column_copy(s, i):
        return pltpu.make_async_remote_copy(
            src_ref=side_out.at[s, i],
            dst_ref=side_in.at[s, 1 - i],
            send_sem=hsend.at[s, 2 + i],
            recv_sem=hrecv.at[s, 3 - i],
            device_id={"lat": lat, "lon": lax.rem(lon + lons + 2 * i - 1, lons)},
            device_id_type=MESH,
        )

    def send_patches(s):
        for o in SENT_FIRST:
            for j in range(CAP):
                snd[s, o, j] = st[s, ti[s * per_step + send0 + o * CAP + j]]

            @pl.when(in_range(OFFSETS[o]))
            def _():
                patch_copy(s, o).start()

    def fractions(s, e):
        return tuple(tf[(s * 3 + i) * np_ + e] for i in range(3))

    def masses(s):
        def send(k, _):
            pltpu.make_async_remote_copy(
                src_ref=mass_out.at[s],
                dst_ref=mass_in.at[s, k],
                send_sem=msend.at[s],
                recv_sem=mrecv.at[s],
                device_id=peer(k),
                device_id_type=MESH,
            ).start()
            return 0

        lax.fori_loop(1, peers, send, 0)

    def masses_sum(s):
        others = mass_in.at[s, pl.ds(1, peers - 1)]
        pltpu.make_async_copy(others, others, mrecv.at[s]).wait()
        return jnp.sum(mass_in[s], axis=0)

    def advect(s, ratio):
        def own(q, _):
            c, r = q // br, lax.rem(q, br)
            e = r * bc + c
            block = st[s, ti[s * per_step + local0 + e]]
            done = interpolate([block[i] for i in range(8)], fractions(s, e), ratio)
            for i in range(8):
                adv[s, c, 1 + r * 8 + i] = done[i]
            return 0

        lax.fori_loop(0, np_, own, 0)
        for o in (1, 2, 0, 3):

            @pl.when(in_range(OFFSETS[o]))
            def _():
                patch_copy(s, 3 - o).wait_recv()

                def come(j, _):
                    e = ti[s * per_step + arrive0 + o * CAP + j]
                    block = arr[s, o, j]
                    done = interpolate(
                        [block[i] for i in range(8)], fractions(s, e), ratio
                    )
                    for i in range(8):
                        ia[s, o * CAP + j, i] = done[i]
                    return 0

                lax.fori_loop(0, CAP, come, 0)

        def join(q, total):
            c, r = q // br, lax.rem(q, br)
            e = r * bc + c
            pick = ti[s * per_step + pick0 + e]
            block = ia[s, jnp.maximum(pick, 0)]
            far = jnp.full((8, values), pick, jnp.int32) >= 0
            for i in range(8):
                v = jnp.where(far, block[i], adv[s, c, 1 + r * 8 + i])
                adv[s, c, 1 + r * 8 + i] = v
                total = total + tf[w0 + r * 8 + i] * v
            return total

        total = lax.fori_loop(0, np_, join, zero)
        for i in range(2):

            @pl.when(in_range(2 * i - 1))
            def _():
                row_copy(s, i).start()

        for i in range(rows):
            side_out[s, 0, i : i + 1] = adv[s, 0, 1 + i][0:1]
            side_out[s, 1, i : i + 1] = adv[s, bc - 1, 1 + i][7:8]
        for i in range(2):
            column_copy(s, i).start()
        first = functools.reduce(jnp.add, [adv[s, c, 1] for c in range(bc)])
        last = functools.reduce(jnp.add, [adv[s, c, rows] for c in range(bc)])
        return total + first * ka_in[0] + last * ka_in[1]

    def wait_halos(s):
        for i in range(2):

            @pl.when(in_range(2 * i - 1))
            def _():
                row_copy(s, 1 - i).wait_recv()

            column_copy(s, 1 - i).wait_recv()

    column = lax.broadcasted_iota(jnp.int32, (8, values), 0)

    def diffused_row(s, row):
        here = [adv[s, c, 1 + row] for c in range(bc)]
        ahead = [pltpu.roll(v, 7, 0) for v in here]
        behind = [pltpu.roll(v, 1, 0) for v in here]
        west = jnp.broadcast_to(side_in[s, 0, pl.ds(row, 1)], (8, values))
        east = jnp.broadcast_to(side_in[s, 1, pl.ds(row, 1)], (8, values))
        kappa = tf[kappa0 + row]
        result = []
        for c in range(bc):
            e = jnp.where(column == 7, east if c == bc - 1 else ahead[c + 1], ahead[c])
            w = jnp.where(column == 0, west if c == 0 else behind[c - 1], behind[c])
            lap = adv[s, c, row] + adv[s, c, row + 2] + e + w - 4.0 * here[c]
            result.append(here[c] + kappa * lap)
        return result

    for i in range(2):

        @pl.when(in_range(2 * i - 1))
        def _():
            ka_copy(i).start()

    for copy in loads:
        copy.wait()

    send_patches(0)

    def target_row(row, total):
        parts = [st[0, c * br + row // 8, lax.rem(row, 8)] for c in range(bc)]
        return total + tf[area0 + row] * functools.reduce(jnp.add, parts)

    target_part = lax.fori_loop(0, rows, target_row, zero)
    for i in range(2):

        @pl.when(in_range(2 * i - 1))
        def _():
            ka_copy(1 - i).wait_recv()

    total = advect(0, None)
    both = jnp.concatenate(
        [
            jnp.sum(total, axis=0, keepdims=True),
            jnp.sum(target_part, axis=0, keepdims=True),
        ],
        axis=0,
    )
    mass_out[0] = both
    mass_in[0, 0] = both
    masses(0)
    wait_halos(0)

    def first_step(row, _):
        done = diffused_row(0, row)
        for c in range(bc):
            st[1, c * br + row // 8, lax.rem(row, 8)] = done[c]
        return 0

    lax.fori_loop(0, rows, first_step, 0)
    send_patches(1)
    sums = masses_sum(0)
    target = sums[1:2]
    ratio = jnp.broadcast_to(target / sums[0:1], (8, values))
    total = advect(1, ratio)
    both = jnp.broadcast_to(jnp.sum(total, axis=0, keepdims=True), (2, values))
    mass_out[1] = both
    mass_in[1, 0] = both
    masses(1)
    wait_halos(1)
    ratio = jnp.broadcast_to(target / masses_sum(1)[0:1], (8, values))

    stores = []
    for r in range(br):

        def last_step(i, _):
            done = diffused_row(1, r * 8 + i)
            for c in range(bc):
                outbuf[r, i, c] = done[c] * ratio
            return 0

        lax.fori_loop(0, 8, last_step, 0)
        copy = pltpu.make_async_copy(outbuf.at[r], out.at[r], store_sem.at[r])
        copy.start()
        stores.append(copy)

    for s in range(STEPS):
        for o in range(4):

            @pl.when(in_range(OFFSETS[o]))
            def _():
                patch_copy(s, o).wait_send()

        for i in range(2):

            @pl.when(in_range(2 * i - 1))
            def _():
                row_copy(s, i).wait_send()

            column_copy(s, i).wait_send()
        others = mass_in.at[s, pl.ds(1, peers - 1)]
        pltpu.make_async_copy(others, others, msend.at[s]).wait()
    for i in range(2):

        @pl.when(in_range(2 * i - 1))
        def _():
            ka_copy(i).wait_send()

    for copy in stores:
        copy.wait()


def tables(source_patch, shifts, diffusivity, br, bc, rows):
    lats = lax.axis_size("lat")
    lat = lax.axis_index("lat")
    lon = lax.axis_index("lon")
    np_ = br * bc
    total_cols = source_patch.shape[2]
    padded = jnp.pad(
        source_patch, ((0, 0), (2 * br, 2 * br), (0, 0)), constant_values=-1
    )
    near = lax.dynamic_slice(
        padded, (0, lat * br, lon * bc), (STEPS, 5 * br, bc)
    ).reshape(STEPS, 5, np_)
    source_row = near // total_cols
    source_dev = source_row // br
    source_q = (near % total_cols - lon * bc) * br + source_row % br
    entries = jnp.arange(np_)
    earlier = entries[None, :] < entries[:, None]
    same = source_dev[..., :, None] == source_dev[..., None, :]
    rank = jnp.sum((same & earlier).astype(jnp.int32), axis=-1)
    outer = jnp.array([0, 1, 3, 4])
    relative = source_dev[:, 2] - lat
    slots = jnp.arange(CAP)
    from_here = source_dev[:, outer] == lat
    chosen = from_here[..., None] & (rank[:, outer][..., None] == slots)
    send = jnp.sum(jnp.where(chosen, source_q[:, outer][..., None], 0), axis=2)
    arrives = relative[:, None, :] == jnp.array(OFFSETS)[None, :, None]
    chosen = arrives[..., None] & (rank[:, 2][:, None, :, None] == slots)
    arrive = jnp.sum(jnp.where(chosen, entries[None, None, :, None], 0), axis=2)
    is_local = relative == 0
    local = jnp.where(is_local, source_q[:, 2], 0)
    place = jnp.where(relative < 0, relative + 2, relative + 1) * CAP + rank[:, 2]
    pick = jnp.where(is_local, -1, place)
    ti = jnp.concatenate(
        [send.reshape(STEPS, -1), arrive.reshape(STEPS, -1), local, pick], axis=1
    ).reshape(-1)
    mine = lax.dynamic_slice(
        shifts, (0, 0, lat * br, lon * bc), (STEPS, 3, br, bc)
    ).reshape(-1)
    area = column_area(lat * rows, rows, rows * lats)
    ka = diffusivity * area
    w0 = area - 2.0 * ka + jnp.pad(ka[1:], (0, 1)) + jnp.pad(ka[:-1], (1, 0))
    tf = jnp.concatenate([mine, diffusivity, area, w0])
    return ti.astype(jnp.int32), tf


def local(lats, lons, tracers, shifts, diffusivity, source_patch):
    rows, cols, values = tracers.shape
    br, bc = rows // 8, cols // 8
    np_ = br * bc
    ti, tf = tables(source_patch, shifts, diffusivity, br, bc, rows)
    tile = (8, 8, values)
    peers = lats * lons
    dma = pltpu.SemaphoreType.DMA
    f32 = jnp.float32
    result = pl.pallas_call(
        functools.partial(kernel, br, bc, lats, lons),
        out_shape=jax.ShapeDtypeStruct((br, 8, bc, 8, values), f32),
        in_specs=[
            pl.BlockSpec(memory_space=pltpu.SMEM),
            pl.BlockSpec(memory_space=pltpu.SMEM),
            pl.BlockSpec(memory_space=pl.ANY),
        ],
        out_specs=pl.BlockSpec(memory_space=pl.ANY),
        scratch_shapes=[
            pltpu.VMEM((STEPS, np_) + tile, f32),
            pltpu.VMEM((STEPS, 4, CAP) + tile, f32),
            pltpu.VMEM((STEPS, 4 * CAP) + tile, f32),
            pltpu.VMEM((STEPS, 4, CAP) + tile, f32),
            pltpu.VMEM((STEPS, bc, rows + 2, 8, values), f32),
            pltpu.VMEM((br, 8, bc, 8, values), f32),
            pltpu.VMEM((STEPS, 2, rows, values), f32),
            pltpu.VMEM((STEPS, 2, rows, values), f32),
            pltpu.VMEM((2, 1, values), f32),
            pltpu.VMEM((2, 1, values), f32),
            pltpu.VMEM((STEPS, 2, values), f32),
            pltpu.VMEM((STEPS, peers, 2, values), f32),
            dma((bc,)),
            dma((br,)),
            dma((STEPS, 4)),
            dma((STEPS, 4)),
            dma((STEPS, 4)),
            dma((STEPS, 4)),
            dma((2,)),
            dma((2,)),
            dma((STEPS,)),
            dma((STEPS,)),
        ],
        compiler_params=pltpu.CompilerParams(
            collective_id=0, has_side_effects=True, vmem_limit_bytes=32 * 1024 * 1024
        ),
    )(ti, tf, tracers.reshape(br, 8, bc, 8, values))
    return result.reshape(rows, cols, values)


def solution(mesh):
    return jax.shard_map(
        functools.partial(local, mesh.shape["lat"], mesh.shape["lon"]),
        mesh=mesh,
        in_specs=(
            P(("groups", "lat"), "lon", None),
            P("groups", None, None, None),
            P("lat"),
            P("groups", None, None),
        ),
        out_specs=P(("groups", "lat"), "lon", None),
        check_vma=False,
    )
```

```python
import functools
import math

import jax
import jax.numpy as jnp
from jax import lax
from jax.experimental import pallas as pl
from jax.experimental.pallas import tpu as pltpu
from jax.sharding import PartitionSpec as P

LEV = 4
STEPS = 2
CAP = 4
OFFSETS = (-2, -1, 1, 2)
SENT_FIRST = (0, 3, 1, 2)
MESH = pl.DeviceIdType.MESH


def column_area(first_row, row_count, total_rows):
    latitude = ((first_row + jnp.arange(row_count)).astype(jnp.float32) + 0.5) * (
        math.pi / total_rows
    ) - 0.5 * math.pi
    return jnp.cos(latitude)


def cubic_weights(s):
    return (
        -s * (s - 1.0) * (s - 2.0) * (1.0 / 6.0),
        (s + 1.0) * (s - 1.0) * (s - 2.0) * 0.5,
        -(s + 1.0) * s * (s - 2.0) * 0.5,
        (s + 1.0) * s * (s - 1.0) * (1.0 / 6.0),
    )


def place_weights(w, place, last):
    a, b, c, d = w
    return (
        jnp.where(place == 0, 0.0, a),
        b + jnp.where(place == 0, a, 0.0) + jnp.where(place == last, c + d, 0.0),
        jnp.where(place == last, 0.0, c + jnp.where(place == last - 1, d, 0.0)),
        jnp.where(place >= last - 1, 0.0, d),
    )


def interpolate(rows, fractions, ratio):
    values = rows[0].shape[1]
    step = values // LEV
    column = lax.broadcasted_iota(jnp.int32, (8, values), 0)
    level = lax.broadcasted_iota(jnp.int32, (8, values), 1) // step
    sy, sx, sz = (jnp.full((8, values), s, jnp.float32) for s in fractions)
    a, b, c, d = cubic_weights(sy)
    ab, cd = a + b, c + d
    bcd = b + cd
    x = rows
    if ratio is not None:
        x = [r * ratio for r in x]
    out = [ab * x[0] + c * x[1] + d * x[2]]
    for i in range(1, 6):
        out.append(a * x[i - 1] + b * x[i] + c * x[i + 1] + d * x[i + 2])
    out.append(a * x[5] + b * x[6] + cd * x[7])
    out.append(a * x[6] + bcd * x[7])
    wx = place_weights(cubic_weights(sx), column, 7)
    wz = place_weights(cubic_weights(sz), level, LEV - 1)
    done = []
    for v in out:
        v = (
            wx[0] * pltpu.roll(v, 1, 0)
            + wx[1] * v
            + wx[2] * pltpu.roll(v, 7, 0)
            + wx[3] * pltpu.roll(v, 6, 0)
        )
        v = (
            wz[0] * pltpu.roll(v, step, 1)
            + wz[1] * v
            + wz[2] * pltpu.roll(v, values - step, 1)
            + wz[3] * pltpu.roll(v, values - 2 * step, 1)
        )
        done.append(v)
    return done


def several(count, unroll, body, carry):
    def turn(i, carry):
        for k in range(unroll):
            carry = body(i * unroll + k, carry)
        return carry

    return lax.fori_loop(0, count // unroll, turn, carry)


def kernel(
    br, bc, lats, lons,
    ti, tf, tr, out,
    st, arr, ia, snd, adv, side_out, side_in, ka_out, ka_in, mass_out, mass_in,
    load_sem, psend, precv, hsend, hrecv, ksend, krecv, msend, mrecv,
):
    np_ = br * bc
    rows = br * 8
    peers = lats * lons
    values = tr.shape[-1]
    lat = lax.axis_index("lat")
    lon = lax.axis_index("lon")
    kappa0 = STEPS * 3 * np_
    area0 = kappa0 + rows
    w0 = area0 + rows
    send0, arrive0, local0, pick0 = 0, 4 * CAP, 8 * CAP, 8 * CAP + np_
    per_step = 8 * CAP + 2 * np_

    loads = [
        pltpu.make_async_copy(
            tr.at[:, :, c], st.at[0, pl.ds(c * br, br)], load_sem.at[c]
        )
        for c in range(bc)
    ]
    for copy in loads:
        copy.start()

    zero = jnp.zeros((8, values), jnp.float32)
    for s in range(STEPS):
        for c in range(bc):
            adv[s, c, 0] = zero
            adv[s, c, rows + 1] = zero
    ka_in[...] = jnp.zeros_like(ka_in)
    ka_out[0] = jnp.full((1, values), tf[kappa0] * tf[area0], jnp.float32)
    ka_out[1] = jnp.full(
        (1, values), tf[kappa0 + rows - 1] * tf[area0 + rows - 1], jnp.float32
    )

    def peer(k):
        return {
            "lat": lax.rem(lat + k // lons, lats),
            "lon": lax.rem(lon + lax.rem(k, lons), lons),
        }

    barrier = pltpu.get_barrier_semaphore()

    def greet(k, _):
        pl.semaphore_signal(barrier, inc=1, device_id=peer(k), device_id_type=MESH)
        return 0

    lax.fori_loop(1, peers, greet, 0)
    pl.semaphore_wait(barrier, peers - 1)

    def in_range(offset):
        return (lat + offset >= 0) & (lat + offset < lats)

    def patch_copy(s, o):
        return pltpu.make_async_remote_copy(
            src_ref=snd.at[s, o],
            dst_ref=arr.at[s, 3 - o],
            send_sem=psend.at[s, o],
            recv_sem=precv.at[s, 3 - o],
            device_id={"lat": jnp.clip(lat + OFFSETS[o], 0, lats - 1), "lon": lon},
            device_id_type=MESH,
        )

    def ka_copy(i):
        return pltpu.make_async_remote_copy(
            src_ref=ka_out.at[i],
            dst_ref=ka_in.at[1 - i],
            send_sem=ksend.at[i],
            recv_sem=krecv.at[1 - i],
            device_id={"lat": jnp.clip(lat + 2 * i - 1, 0, lats - 1), "lon": lon},
            device_id_type=MESH,
        )

    def row_copy(s, i):
        return pltpu.make_async_remote_copy(
            src_ref=adv.at[s, :, rows if i else 1],
            dst_ref=adv.at[s, :, 0 if i else rows + 1],
            send_sem=hsend.at[s, i],
            recv_sem=hrecv.at[s, 1 - i],
            device_id={"lat": jnp.clip(lat + 2 * i - 1, 0, lats - 1), "lon": lon},
            device_id_type=MESH,
        )

    def column_copy(s, i):
        return pltpu.make_async_remote_copy(
            src_ref=side_out.at[s, i],
            dst_ref=side_in.at[s, 1 - i],
            send_sem=hsend.at[s, 2 + i],
            recv_sem=hrecv.at[s, 3 - i],
            device_id={"lat": lat, "lon": lax.rem(lon + lons + 2 * i - 1, lons)},
            device_id_type=MESH,
        )

    def send_patches(s):
        for o in SENT_FIRST:
            for j in range(CAP):
                snd[s, o, j] = st[s, ti[s * per_step + send0 + o * CAP + j]]

            @pl.when(in_range(OFFSETS[o]))
            def _():
                patch_copy(s, o).start()

    def fractions(s, e):
        return tuple(tf[(s * 3 + i) * np_ + e] for i in range(3))

    def masses(s):
        def send(k, _):
            pltpu.make_async_remote_copy(
                src_ref=mass_out.at[s],
                dst_ref=mass_in.at[s, k],
                send_sem=msend.at[s],
                recv_sem=mrecv.at[s],
                device_id=peer(k),
                device_id_type=MESH,
            ).start()
            return 0

        lax.fori_loop(1, peers, send, 0)

    def masses_sum(s):
        others = mass_in.at[s, pl.ds(1, peers - 1)]
        pltpu.make_async_copy(others, others, mrecv.at[s]).wait()
        return jnp.sum(mass_in[s], axis=0)

    def advect(s, ratio):
        def own(q, _):
            c, r = q // br, lax.rem(q, br)
            e = r * bc + c
            block = st[s, ti[s * per_step + local0 + e]]
            done = interpolate([block[i] for i in range(8)], fractions(s, e), ratio)
            for i in range(8):
                adv[s, c, 1 + r * 8 + i] = done[i]
            return 0

        several(np_, 4, own, 0)
        for o in (1, 2, 0, 3):

            @pl.when(in_range(OFFSETS[o]))
            def _():
                patch_copy(s, 3 - o).wait_recv()

                def come(j, _):
                    e = ti[s * per_step + arrive0 + o * CAP + j]
                    block = arr[s, o, j]
                    done = interpolate(
                        [block[i] for i in range(8)], fractions(s, e), ratio
                    )
                    for i in range(8):
                        ia[s, o * CAP + j, i] = done[i]
                    return 0

                several(CAP, CAP, come, 0)

        def join(q, total):
            c, r = q // br, lax.rem(q, br)
            e = r * bc + c
            pick = ti[s * per_step + pick0 + e]
            block = ia[s, jnp.maximum(pick, 0)]
            far = jnp.full((8, values), pick, jnp.int32) >= 0
            for i in range(8):
                v = jnp.where(far, block[i], adv[s, c, 1 + r * 8 + i])
                adv[s, c, 1 + r * 8 + i] = v
                total = total + tf[w0 + r * 8 + i] * v
            return total

        total = several(np_, 4, join, zero)
        for i in range(2):

            @pl.when(in_range(2 * i - 1))
            def _():
                row_copy(s, i).start()

        for i in range(rows):
            side_out[s, 0, i : i + 1] = adv[s, 0, 1 + i][0:1]
            side_out[s, 1, i : i + 1] = adv[s, bc - 1, 1 + i][7:8]
        for i in range(2):
            column_copy(s, i).start()
        first = functools.reduce(jnp.add, [adv[s, c, 1] for c in range(bc)])
        last = functools.reduce(jnp.add, [adv[s, c, rows] for c in range(bc)])
        return total + first * ka_in[0] + last * ka_in[1]

    def wait_halos(s):
        for i in range(2):

            @pl.when(in_range(2 * i - 1))
            def _():
                row_copy(s, 1 - i).wait_recv()

            column_copy(s, 1 - i).wait_recv()

    column = lax.broadcasted_iota(jnp.int32, (8, values), 0)

    def diffused_row(s, row):
        here = [adv[s, c, 1 + row] for c in range(bc)]
        ahead = [pltpu.roll(v, 7, 0) for v in here]
        behind = [pltpu.roll(v, 1, 0) for v in here]
        west = jnp.broadcast_to(side_in[s, 0, pl.ds(row, 1)], (8, values))
        east = jnp.broadcast_to(side_in[s, 1, pl.ds(row, 1)], (8, values))
        kappa = tf[kappa0 + row]
        result = []
        for c in range(bc):
            e = jnp.where(column == 7, east if c == bc - 1 else ahead[c + 1], ahead[c])
            w = jnp.where(column == 0, west if c == 0 else behind[c - 1], behind[c])
            lap = adv[s, c, row] + adv[s, c, row + 2] + e + w - 4.0 * here[c]
            result.append(here[c] + kappa * lap)
        return result

    for i in range(2):

        @pl.when(in_range(2 * i - 1))
        def _():
            ka_copy(i).start()

    for copy in loads:
        copy.wait()

    send_patches(0)

    def target_row(row, total):
        parts = [st[0, c * br + row // 8, lax.rem(row, 8)] for c in range(bc)]
        return total + tf[area0 + row] * functools.reduce(jnp.add, parts)

    target_part = several(rows, 4, target_row, zero)
    for i in range(2):

        @pl.when(in_range(2 * i - 1))
        def _():
            ka_copy(1 - i).wait_recv()

    total = advect(0, None)
    both = jnp.concatenate(
        [
            jnp.sum(total, axis=0, keepdims=True),
            jnp.sum(target_part, axis=0, keepdims=True),
        ],
        axis=0,
    )
    mass_out[0] = both
    mass_in[0, 0] = both
    masses(0)
    wait_halos(0)

    def first_step(row, _):
        done = diffused_row(0, row)
        for c in range(bc):
            st[1, c * br + row // 8, lax.rem(row, 8)] = done[c]
        return 0

    several(rows, 4, first_step, 0)
    send_patches(1)
    sums = masses_sum(0)
    target = sums[1:2]
    ratio = jnp.broadcast_to(target / sums[0:1], (8, values))
    total = advect(1, ratio)
    both = jnp.broadcast_to(jnp.sum(total, axis=0, keepdims=True), (2, values))
    mass_out[1] = both
    mass_in[1, 0] = both
    masses(1)
    wait_halos(1)
    ratio = jnp.broadcast_to(target / masses_sum(1)[0:1], (8, values))

    def last_step(row, _):
        done = diffused_row(1, row)
        for c in range(bc):
            out[row // 8, lax.rem(row, 8), c] = done[c] * ratio
        return 0

    several(rows, 4, last_step, 0)

    for s in range(STEPS):
        for o in range(4):

            @pl.when(in_range(OFFSETS[o]))
            def _():
                patch_copy(s, o).wait_send()

        for i in range(2):

            @pl.when(in_range(2 * i - 1))
            def _():
                row_copy(s, i).wait_send()

            column_copy(s, i).wait_send()
        others = mass_in.at[s, pl.ds(1, peers - 1)]
        pltpu.make_async_copy(others, others, msend.at[s]).wait()
    for i in range(2):

        @pl.when(in_range(2 * i - 1))
        def _():
            ka_copy(i).wait_send()


def tables(source_patch, shifts, diffusivity, br, bc, rows):
    lats = lax.axis_size("lat")
    lat = lax.axis_index("lat")
    lon = lax.axis_index("lon")
    np_ = br * bc
    total_cols = source_patch.shape[2]
    padded = jnp.pad(
        source_patch, ((0, 0), (2 * br, 2 * br), (0, 0)), constant_values=-1
    )
    near = lax.dynamic_slice(
        padded, (0, lat * br, lon * bc), (STEPS, 5 * br, bc)
    ).reshape(STEPS, 5, np_)
    source_row = near // total_cols
    source_dev = source_row // br
    source_q = (near % total_cols - lon * bc) * br + source_row % br
    entries = jnp.arange(np_)
    earlier = entries[None, :] < entries[:, None]
    same = source_dev[..., :, None] == source_dev[..., None, :]
    rank = jnp.sum((same & earlier).astype(jnp.int32), axis=-1)
    outer = jnp.array([0, 1, 3, 4])
    relative = source_dev[:, 2] - lat
    slots = jnp.arange(CAP)
    from_here = source_dev[:, outer] == lat
    chosen = from_here[..., None] & (rank[:, outer][..., None] == slots)
    send = jnp.sum(jnp.where(chosen, source_q[:, outer][..., None], 0), axis=2)
    arrives = relative[:, None, :] == jnp.array(OFFSETS)[None, :, None]
    chosen = arrives[..., None] & (rank[:, 2][:, None, :, None] == slots)
    arrive = jnp.sum(jnp.where(chosen, entries[None, None, :, None], 0), axis=2)
    is_local = relative == 0
    local = jnp.where(is_local, source_q[:, 2], 0)
    place = jnp.where(relative < 0, relative + 2, relative + 1) * CAP + rank[:, 2]
    pick = jnp.where(is_local, -1, place)
    ti = jnp.concatenate(
        [send.reshape(STEPS, -1), arrive.reshape(STEPS, -1), local, pick], axis=1
    ).reshape(-1)
    mine = lax.dynamic_slice(
        shifts, (0, 0, lat * br, lon * bc), (STEPS, 3, br, bc)
    ).reshape(-1)
    area = column_area(lat * rows, rows, rows * lats)
    ka = diffusivity * area
    w0 = area - 2.0 * ka + jnp.pad(ka[1:], (0, 1)) + jnp.pad(ka[:-1], (1, 0))
    tf = jnp.concatenate([mine, diffusivity, area, w0])
    return ti.astype(jnp.int32), tf


def local(lats, lons, tracers, shifts, diffusivity, source_patch):
    rows, cols, values = tracers.shape
    br, bc = rows // 8, cols // 8
    np_ = br * bc
    ti, tf = tables(source_patch, shifts, diffusivity, br, bc, rows)
    tile = (8, 8, values)
    peers = lats * lons
    dma = pltpu.SemaphoreType.DMA
    f32 = jnp.float32
    result = pl.pallas_call(
        functools.partial(kernel, br, bc, lats, lons),
        out_shape=pltpu.VMEM((br, 8, bc, 8, values), f32),
        in_specs=[
            pl.BlockSpec(memory_space=pltpu.SMEM),
            pl.BlockSpec(memory_space=pltpu.SMEM),
            pl.BlockSpec(memory_space=pltpu.HBM),
        ],
        out_specs=pl.BlockSpec(memory_space=pltpu.VMEM),
        scratch_shapes=[
            pltpu.VMEM((STEPS, np_) + tile, f32),
            pltpu.VMEM((STEPS, 4, CAP) + tile, f32),
            pltpu.VMEM((STEPS, 4 * CAP) + tile, f32),
            pltpu.VMEM((STEPS, 4, CAP) + tile, f32),
            pltpu.VMEM((STEPS, bc, rows + 2, 8, values), f32),
            pltpu.VMEM((STEPS, 2, rows, values), f32),
            pltpu.VMEM((STEPS, 2, rows, values), f32),
            pltpu.VMEM((2, 1, values), f32),
            pltpu.VMEM((2, 1, values), f32),
            pltpu.VMEM((STEPS, 2, values), f32),
            pltpu.VMEM((STEPS, peers, 2, values), f32),
            dma((bc,)),
            dma((STEPS, 4)),
            dma((STEPS, 4)),
            dma((STEPS, 4)),
            dma((STEPS, 4)),
            dma((2,)),
            dma((2,)),
            dma((STEPS,)),
            dma((STEPS,)),
        ],
        compiler_params=pltpu.CompilerParams(
            collective_id=0, has_side_effects=True, vmem_limit_bytes=32 * 1024 * 1024
        ),
    )(ti, tf, tracers.reshape(br, 8, bc, 8, values))
    return result.reshape(rows, cols, values)


def solution(mesh):
    return jax.shard_map(
        functools.partial(local, mesh.shape["lat"], mesh.shape["lon"]),
        mesh=mesh,
        in_specs=(
            P(("groups", "lat"), "lon", None),
            P("groups", None, None, None),
            P("lat"),
            P("groups", None, None),
        ),
        out_specs=P(("groups", "lat"), "lon", None),
        check_vma=False,
    )
```

```python
import functools
import math

import jax
import jax.numpy as jnp
from jax import lax
from jax.experimental import pallas as pl
from jax.experimental.pallas import tpu as pltpu
from jax.sharding import PartitionSpec as P

LEV = 4
STEPS = 2
CAP = 4
OFFSETS = (-2, -1, 1, 2)
SENT_FIRST = (0, 3, 1, 2)
MESH = pl.DeviceIdType.MESH


def cubic_weights(s):
    return (
        -s * (s - 1.0) * (s - 2.0) * (1.0 / 6.0),
        (s + 1.0) * (s - 1.0) * (s - 2.0) * 0.5,
        -(s + 1.0) * s * (s - 2.0) * 0.5,
        (s + 1.0) * s * (s - 1.0) * (1.0 / 6.0),
    )


def place_weights(w, place, last):
    a, b, c, d = w
    return (
        jnp.where(place == 0, 0.0, a),
        b + jnp.where(place == 0, a, 0.0) + jnp.where(place == last, c + d, 0.0),
        jnp.where(place == last, 0.0, c + jnp.where(place == last - 1, d, 0.0)),
        jnp.where(place >= last - 1, 0.0, d),
    )


def interpolate(rows, weights, ratio):
    values = rows[0].shape[1]
    step = values // LEV
    column = lax.broadcasted_iota(jnp.int32, (8, values), 0)
    level = lax.broadcasted_iota(jnp.int32, (8, values), 1) // step
    wy, wx, wz = (
        [jnp.full((8, values), w, jnp.float32) for w in part] for part in weights
    )
    a, b, c, d = wy
    ab, cd = a + b, c + d
    bcd = b + cd
    x = rows
    if ratio is not None:
        x = [r * ratio for r in x]
    out = [ab * x[0] + c * x[1] + d * x[2]]
    for i in range(1, 6):
        out.append(a * x[i - 1] + b * x[i] + c * x[i + 1] + d * x[i + 2])
    out.append(a * x[5] + b * x[6] + cd * x[7])
    out.append(a * x[6] + bcd * x[7])
    wx = place_weights(wx, column, 7)
    wz = place_weights(wz, level, LEV - 1)
    done = []
    for v in out:
        v = (
            wx[0] * pltpu.roll(v, 1, 0)
            + wx[1] * v
            + wx[2] * pltpu.roll(v, 7, 0)
            + wx[3] * pltpu.roll(v, 6, 0)
        )
        v = (
            wz[0] * pltpu.roll(v, step, 1)
            + wz[1] * v
            + wz[2] * pltpu.roll(v, values - step, 1)
            + wz[3] * pltpu.roll(v, values - 2 * step, 1)
        )
        done.append(v)
    return done


def quotient(x, n):
    if n & (n - 1) == 0:
        return lax.shift_right_logical(x, jnp.full_like(x, n.bit_length() - 1))
    return lax.div(x, jnp.full_like(x, n))


def make_tables(br, bc, lats, lat, lon, source, shift, near, near_shift, ti, tf):
    np_ = br * bc
    rows = br * 8
    lat_rows, total_cols = source.shape[1:]
    lanes = ti.shape[1]
    lane = lax.broadcasted_iota(jnp.int32, (8, lanes), 1)
    sub = lax.broadcasted_iota(jnp.int32, (8, lanes), 0)
    at = lax.broadcasted_iota(jnp.int32, (total_cols, lanes), 0)
    entry = lax.broadcasted_iota(jnp.int32, (total_cols, lanes), 1)
    pick_columns = jnp.where(at == lon * bc + entry % bc, 1.0, 0.0)
    near[...] = jnp.dot(
        source[...].reshape(STEPS * lat_rows, total_cols).astype(jnp.float32),
        pick_columns,
        precision=lax.Precision.HIGHEST,
        preferred_element_type=jnp.float32,
    )
    near_shift[...] = jnp.dot(
        shift[...].reshape(STEPS * 3 * lat_rows, total_cols),
        pick_columns,
        precision=lax.Precision.HIGHEST,
        preferred_element_type=jnp.float32,
    )
    row_of = lax.broadcasted_iota(jnp.int32, (br, lanes), 1) // bc
    own_row = row_of == lax.broadcasted_iota(jnp.int32, (br, lanes), 0)

    def band(ref, first):
        block = ref[pl.ds(first, br), :]
        return jnp.sum(jnp.where(own_row, block, 0.0), axis=0, keepdims=True)

    parts = [band(near_shift, k * lat_rows + lat * br) for k in range(STEPS * 3)]
    parts += [parts[0]] * (8 - STEPS * 3)
    for k, w in enumerate(cubic_weights(jnp.concatenate(parts, axis=0))):
        tf[8 * k : 8 * k + 8, :] = w
    latitude = ((lat * rows + lane).astype(jnp.float32) + 0.5) * (
        math.pi / (rows * lats)
    ) - 0.5 * math.pi
    tf[32:40, :] = jnp.cos(latitude)

    valid = lane < np_
    dest = jnp.clip(lat + jnp.minimum(sub, 4) - 2, 0, lats - 1)
    own_rows = []
    for s in range(STEPS):
        places = [
            s * lat_rows + jnp.clip(lat + o, 0, lats - 1) * br for o in range(-2, 3)
        ]
        bands = [band(near, p) for p in places]
        bands += [bands[4]] * 3
        ids = jnp.concatenate(bands, axis=0).astype(jnp.int32)
        source_row = quotient(ids, total_cols)
        source_dev = quotient(source_row, br)
        source_q = (ids - source_row * total_cols - lon * bc) * br + (
            source_row - source_dev * br
        )
        relative = source_dev - dest + 2
        count = jnp.zeros((8, lanes), jnp.int32)
        for k in range(5):
            count = jnp.where((relative == k) & valid, 1 << (6 * k), count)
        reach = 1
        while reach < np_:
            count = count + jnp.where(lane >= reach, pltpu.roll(count, reach, 1), 0)
            reach *= 2
        rank = jnp.zeros((8, lanes), jnp.int32)
        for k in range(5):
            field = lax.shift_right_logical(count, jnp.full_like(count, 6 * k))
            rank = jnp.where(relative == k, (field & 63) - 1, rank)
        code = jnp.where((source_dev == lat) & valid, rank, -1)

        def spread(x, picks):
            return jnp.concatenate(
                [jnp.broadcast_to(x[p : p + 1], (CAP, lanes)) for p in picks], axis=0
            )

        outer = (0, 1, 3, 4)
        slot = lax.broadcasted_iota(jnp.int32, (4 * CAP, lanes), 0)
        which = slot // CAP
        which = jnp.where(which >= 2, which + 1, which)
        slot = slot % CAP
        place = lax.broadcasted_iota(jnp.int32, (4 * CAP, lanes), 1)
        sent = jnp.where(spread(code, outer) == slot, spread(source_q, outer), 0)
        mine = (2,) * 4
        hit = (spread(relative, mine) == which) & (spread(rank, mine) == slot)
        come = jnp.where(hit & (place < np_), place, 0)
        sent = jnp.sum(sent.astype(jnp.float32), axis=1, keepdims=True)
        come = jnp.sum(come.astype(jnp.float32), axis=1, keepdims=True)
        ti[s * 4 * CAP : (s + 1) * 4 * CAP, :] = jnp.clip(
            jnp.where(place == 0, sent, come).astype(jnp.int32), 0, np_ - 1
        )
        here = relative == 2
        outer_place = jnp.where(relative > 2, relative - 1, relative) * CAP + rank
        own_rows.append(jnp.clip(jnp.where(here & valid, source_q, 0), 0, np_ - 1)[2:3])
        outer_place = jnp.clip(outer_place, 0, 4 * CAP - 1)
        own_rows.append(jnp.where(here | ~valid, -1, outer_place)[2:3])
    own_rows += own_rows[:1] * (8 - len(own_rows))
    ti[STEPS * 4 * CAP :, :] = jnp.concatenate(own_rows, axis=0)


def several(count, unroll, body, carry):
    def turn(i, carry):
        for k in range(unroll):
            carry = body(i * unroll + k, carry)
        return carry

    return lax.fori_loop(0, count // unroll, turn, carry)


def kernel(
    br, bc, lats, lons,
    source_hbm, shift_hbm, kappa_hbm, tr, out,
    st, arr, ia, snd, adv, side_out, side_in, ka_out, ka_in, mass_out, mass_in,
    source, shift, near, near_shift, ti_v, tf_v, ti, tf, kappa, weight,
    load_sem, small_sem, psend, precv, hsend, hrecv, ksend, krecv, msend, mrecv,
):
    np_ = br * bc
    rows = br * 8
    peers = lats * lons
    values = tr.shape[-1]
    lat = lax.axis_index("lat")
    lon = lax.axis_index("lon")

    small = [
        pltpu.make_async_copy(source_hbm, source, small_sem.at[0]),
        pltpu.make_async_copy(shift_hbm, shift, small_sem.at[1]),
        pltpu.make_async_copy(kappa_hbm, kappa, small_sem.at[2]),
    ]
    for copy in small:
        copy.start()
    loads = [
        pltpu.make_async_copy(
            tr.at[:, :, c], st.at[0, pl.ds(c * br, br)], load_sem.at[c]
        )
        for c in range(bc)
    ]
    for copy in loads:
        copy.start()

    zero = jnp.zeros((8, values), jnp.float32)
    for s in range(STEPS):
        for c in range(bc):
            adv[s, c, 0] = zero
            adv[s, c, rows + 1] = zero
    ka_in[...] = jnp.zeros_like(ka_in)

    def peer(k):
        return {
            "lat": lax.rem(lat + k // lons, lats),
            "lon": lax.rem(lon + lax.rem(k, lons), lons),
        }

    barrier = pltpu.get_barrier_semaphore()

    def greet(k, _):
        pl.semaphore_signal(barrier, inc=1, device_id=peer(k), device_id_type=MESH)
        return 0

    lax.fori_loop(1, peers, greet, 0)
    for copy in small:
        copy.wait()
    make_tables(
        br, bc, lats, lat, lon, source, shift, near, near_shift, ti_v, tf_v
    )
    to_scalar = [
        pltpu.make_async_copy(ti_v, ti, small_sem.at[3]),
        pltpu.make_async_copy(tf_v, tf, small_sem.at[4]),
    ]
    for copy in to_scalar:
        copy.start()
    for copy in to_scalar:
        copy.wait()

    def area(row):
        return tf[32, row]

    for i, row in enumerate((0, rows - 1)):
        ka_out[i] = jnp.full((1, values), kappa[row] * area(row), jnp.float32)
    pl.semaphore_wait(barrier, peers - 1)

    def in_range(offset):
        return (lat + offset >= 0) & (lat + offset < lats)

    def patch_copy(s, o):
        return pltpu.make_async_remote_copy(
            src_ref=snd.at[s, o],
            dst_ref=arr.at[s, 3 - o],
            send_sem=psend.at[s, o],
            recv_sem=precv.at[s, 3 - o],
            device_id={"lat": jnp.clip(lat + OFFSETS[o], 0, lats - 1), "lon": lon},
            device_id_type=MESH,
        )

    def ka_copy(i):
        return pltpu.make_async_remote_copy(
            src_ref=ka_out.at[i],
            dst_ref=ka_in.at[1 - i],
            send_sem=ksend.at[i],
            recv_sem=krecv.at[1 - i],
            device_id={"lat": jnp.clip(lat + 2 * i - 1, 0, lats - 1), "lon": lon},
            device_id_type=MESH,
        )

    def row_copy(s, i):
        return pltpu.make_async_remote_copy(
            src_ref=adv.at[s, :, rows if i else 1],
            dst_ref=adv.at[s, :, 0 if i else rows + 1],
            send_sem=hsend.at[s, i],
            recv_sem=hrecv.at[s, 1 - i],
            device_id={"lat": jnp.clip(lat + 2 * i - 1, 0, lats - 1), "lon": lon},
            device_id_type=MESH,
        )

    def column_copy(s, i):
        return pltpu.make_async_remote_copy(
            src_ref=side_out.at[s, i],
            dst_ref=side_in.at[s, 1 - i],
            send_sem=hsend.at[s, 2 + i],
            recv_sem=hrecv.at[s, 3 - i],
            device_id={"lat": lat, "lon": lax.rem(lon + lons + 2 * i - 1, lons)},
            device_id_type=MESH,
        )

    def send_patches(s):
        for o in SENT_FIRST:
            for j in range(CAP):
                snd[s, o, j] = st[s, ti[(s * 4 + o) * CAP + j, 0]]

            @pl.when(in_range(OFFSETS[o]))
            def _():
                patch_copy(s, o).start()

    def weights(s, e):
        return [[tf[8 * k + s * 3 + i, e] for k in range(4)] for i in range(3)]

    def masses(s):
        def send(k, _):
            pltpu.make_async_remote_copy(
                src_ref=mass_out.at[s],
                dst_ref=mass_in.at[s, k],
                send_sem=msend.at[s],
                recv_sem=mrecv.at[s],
                device_id=peer(k),
                device_id_type=MESH,
            ).start()
            return 0

        lax.fori_loop(1, peers, send, 0)

    def masses_sum(s):
        others = mass_in.at[s, pl.ds(1, peers - 1)]
        pltpu.make_async_copy(others, others, mrecv.at[s]).wait()
        return jnp.sum(mass_in[s], axis=0)

    def advect(s, ratio):
        def own(q, _):
            c, r = q // br, lax.rem(q, br)
            e = r * bc + c
            block = st[s, ti[STEPS * 4 * CAP + 2 * s, e]]
            done = interpolate([block[i] for i in range(8)], weights(s, e), ratio)
            for i in range(8):
                adv[s, c, 1 + r * 8 + i] = done[i]
            return 0

        several(np_, 4, own, 0)
        for o in (1, 2, 0, 3):

            @pl.when(in_range(OFFSETS[o]))
            def _():
                patch_copy(s, 3 - o).wait_recv()

                def come(j, _):
                    e = ti[(s * 4 + o) * CAP + j, 1]
                    block = arr[s, o, j]
                    done = interpolate(
                        [block[i] for i in range(8)], weights(s, e), ratio
                    )
                    for i in range(8):
                        ia[s, o * CAP + j, i] = done[i]
                    return 0

                several(CAP, CAP, come, 0)

        def join(q, total):
            c, r = q // br, lax.rem(q, br)
            e = r * bc + c
            pick = ti[STEPS * 4 * CAP + 2 * s + 1, e]
            block = ia[s, jnp.maximum(pick, 0)]
            far = jnp.full((8, values), pick, jnp.int32) >= 0
            for i in range(8):
                v = jnp.where(far, block[i], adv[s, c, 1 + r * 8 + i])
                adv[s, c, 1 + r * 8 + i] = v
                total = total + weight[r * 8 + i] * v
            return total

        total = several(np_, 4, join, zero)
        for i in range(2):

            @pl.when(in_range(2 * i - 1))
            def _():
                row_copy(s, i).start()

        for i in range(rows):
            side_out[s, 0, i : i + 1] = adv[s, 0, 1 + i][0:1]
            side_out[s, 1, i : i + 1] = adv[s, bc - 1, 1 + i][7:8]
        for i in range(2):
            column_copy(s, i).start()
        first = functools.reduce(jnp.add, [adv[s, c, 1] for c in range(bc)])
        last = functools.reduce(jnp.add, [adv[s, c, rows] for c in range(bc)])
        return total + first * ka_in[0] + last * ka_in[1]

    def wait_halos(s):
        for i in range(2):

            @pl.when(in_range(2 * i - 1))
            def _():
                row_copy(s, 1 - i).wait_recv()

            column_copy(s, 1 - i).wait_recv()

    column = lax.broadcasted_iota(jnp.int32, (8, values), 0)

    def diffused_row(s, row):
        here = [adv[s, c, 1 + row] for c in range(bc)]
        ahead = [pltpu.roll(v, 7, 0) for v in here]
        behind = [pltpu.roll(v, 1, 0) for v in here]
        west = jnp.broadcast_to(side_in[s, 0, pl.ds(row, 1)], (8, values))
        east = jnp.broadcast_to(side_in[s, 1, pl.ds(row, 1)], (8, values))
        number = kappa[row]
        result = []
        for c in range(bc):
            e = jnp.where(column == 7, east if c == bc - 1 else ahead[c + 1], ahead[c])
            w = jnp.where(column == 0, west if c == 0 else behind[c - 1], behind[c])
            lap = adv[s, c, row] + adv[s, c, row + 2] + e + w - 4.0 * here[c]
            result.append(here[c] + number * lap)
        return result

    for i in range(2):

        @pl.when(in_range(2 * i - 1))
        def _():
            ka_copy(i).start()

    for copy in loads:
        copy.wait()

    send_patches(0)

    for row in range(rows):
        w = area(row) * (1.0 - 2.0 * kappa[row])
        if row:
            w = w + area(row - 1) * kappa[row - 1]
        if row < rows - 1:
            w = w + area(row + 1) * kappa[row + 1]
        weight[row] = w

    def target_row(row, total):
        parts = [st[0, c * br + row // 8, lax.rem(row, 8)] for c in range(bc)]
        return total + area(row) * functools.reduce(jnp.add, parts)

    target_part = several(rows, 4, target_row, zero)
    for i in range(2):

        @pl.when(in_range(2 * i - 1))
        def _():
            ka_copy(1 - i).wait_recv()

    total = advect(0, None)
    both = jnp.concatenate(
        [
            jnp.sum(total, axis=0, keepdims=True),
            jnp.sum(target_part, axis=0, keepdims=True),
        ],
        axis=0,
    )
    mass_out[0] = both
    mass_in[0, 0] = both
    masses(0)
    wait_halos(0)

    def first_step(row, _):
        done = diffused_row(0, row)
        for c in range(bc):
            st[1, c * br + row // 8, lax.rem(row, 8)] = done[c]
        return 0

    several(rows, 4, first_step, 0)
    send_patches(1)
    sums = masses_sum(0)
    target = sums[1:2]
    ratio = jnp.broadcast_to(target / sums[0:1], (8, values))
    total = advect(1, ratio)
    both = jnp.broadcast_to(jnp.sum(total, axis=0, keepdims=True), (2, values))
    mass_out[1] = both
    mass_in[1, 0] = both
    masses(1)
    wait_halos(1)
    ratio = jnp.broadcast_to(target / masses_sum(1)[0:1], (8, values))

    def last_step(row, _):
        done = diffused_row(1, row)
        for c in range(bc):
            out[row // 8, lax.rem(row, 8), c] = done[c] * ratio
        return 0

    several(rows, 4, last_step, 0)

    for s in range(STEPS):
        for o in range(4):

            @pl.when(in_range(OFFSETS[o]))
            def _():
                patch_copy(s, o).wait_send()

        for i in range(2):

            @pl.when(in_range(2 * i - 1))
            def _():
                row_copy(s, i).wait_send()

            column_copy(s, i).wait_send()
        others = mass_in.at[s, pl.ds(1, peers - 1)]
        pltpu.make_async_copy(others, others, msend.at[s]).wait()
    for i in range(2):

        @pl.when(in_range(2 * i - 1))
        def _():
            ka_copy(i).wait_send()


def local(lats, lons, tracers, shifts, diffusivity, source_patch):
    rows, cols, values = tracers.shape
    br, bc = rows // 8, cols // 8
    np_ = br * bc
    tile = (8, 8, values)
    peers = lats * lons
    dma = pltpu.SemaphoreType.DMA
    f32 = jnp.float32
    result = pl.pallas_call(
        functools.partial(kernel, br, bc, lats, lons),
        out_shape=pltpu.VMEM((br, 8, bc, 8, values), f32),
        in_specs=[
            pl.BlockSpec(memory_space=pltpu.HBM),
            pl.BlockSpec(memory_space=pltpu.HBM),
            pl.BlockSpec(memory_space=pltpu.HBM),
            pl.BlockSpec(memory_space=pltpu.HBM),
        ],
        out_specs=pl.BlockSpec(memory_space=pltpu.VMEM),
        scratch_shapes=[
            pltpu.VMEM((STEPS, np_) + tile, f32),
            pltpu.VMEM((STEPS, 4, CAP) + tile, f32),
            pltpu.VMEM((STEPS, 4 * CAP) + tile, f32),
            pltpu.VMEM((STEPS, 4, CAP) + tile, f32),
            pltpu.VMEM((STEPS, bc, rows + 2, 8, values), f32),
            pltpu.VMEM((STEPS, 2, rows, values), f32),
            pltpu.VMEM((STEPS, 2, rows, values), f32),
            pltpu.VMEM((2, 1, values), f32),
            pltpu.VMEM((2, 1, values), f32),
            pltpu.VMEM((STEPS, 2, values), f32),
            pltpu.VMEM((STEPS, peers, 2, values), f32),
            pltpu.VMEM(source_patch.shape, jnp.int32),
            pltpu.VMEM(shifts.shape, f32),
            pltpu.VMEM((STEPS * source_patch.shape[1], 128), f32),
            pltpu.VMEM((STEPS * 3 * source_patch.shape[1], 128), f32),
            pltpu.VMEM((STEPS * 4 * CAP + 8, 128), jnp.int32),
            pltpu.VMEM((40, 128), f32),
            pltpu.SMEM((STEPS * 4 * CAP + 8, 128), jnp.int32),
            pltpu.SMEM((40, 128), f32),
            pltpu.SMEM((rows,), f32),
            pltpu.SMEM((rows,), f32),
            dma((bc,)),
            dma((5,)),
            dma((STEPS, 4)),
            dma((STEPS, 4)),
            dma((STEPS, 4)),
            dma((STEPS, 4)),
            dma((2,)),
            dma((2,)),
            dma((STEPS,)),
            dma((STEPS,)),
        ],
        compiler_params=pltpu.CompilerParams(
            collective_id=0, has_side_effects=True, vmem_limit_bytes=32 * 1024 * 1024
        ),
    )(
        *(
            pltpu.with_memory_space_constraint(x, pltpu.HBM)
            for x in (
                source_patch,
                shifts,
                diffusivity,
                tracers.reshape(br, 8, bc, 8, values),
            )
        )
    )
    return result.reshape(rows, cols, values)


def solution(mesh):
    return jax.shard_map(
        functools.partial(local, mesh.shape["lat"], mesh.shape["lon"]),
        mesh=mesh,
        in_specs=(
            P(("groups", "lat"), "lon", None),
            P("groups", None, None, None),
            P("lat"),
            P("groups", None, None),
        ),
        out_specs=P(("groups", "lat"), "lon", None),
        check_vma=False,
    )
```

```python
import functools
import math

import jax
import jax.numpy as jnp
from jax import lax
from jax.experimental import pallas as pl
from jax.experimental.pallas import tpu as pltpu
from jax.sharding import PartitionSpec as P

LEV = 4
STEPS = 2
CAP = 4
OFFSETS = (-2, -1, 1, 2)
SENT_FIRST = (0, 3, 1, 2)
PIECES = 2
PIECE = CAP // PIECES
MESH = pl.DeviceIdType.MESH


def cubic_weights(s):
    return (
        -s * (s - 1.0) * (s - 2.0) * (1.0 / 6.0),
        (s + 1.0) * (s - 1.0) * (s - 2.0) * 0.5,
        -(s + 1.0) * s * (s - 2.0) * 0.5,
        (s + 1.0) * s * (s - 1.0) * (1.0 / 6.0),
    )


def place_weights(w, place, last):
    a, b, c, d = w
    return (
        jnp.where(place == 0, 0.0, a),
        b + jnp.where(place == 0, a, 0.0) + jnp.where(place == last, c + d, 0.0),
        jnp.where(place == last, 0.0, c + jnp.where(place == last - 1, d, 0.0)),
        jnp.where(place >= last - 1, 0.0, d),
    )


def interpolate(rows, weights, ratio):
    values = rows[0].shape[1]
    step = values // LEV
    column = lax.broadcasted_iota(jnp.int32, (8, values), 0)
    level = lax.broadcasted_iota(jnp.int32, (8, values), 1) // step
    wy, wx, wz = (
        [jnp.full((8, values), w, jnp.float32) for w in part] for part in weights
    )
    a, b, c, d = wy
    ab, cd = a + b, c + d
    bcd = b + cd
    x = rows
    if ratio is not None:
        x = [r * ratio for r in x]
    out = [ab * x[0] + c * x[1] + d * x[2]]
    for i in range(1, 6):
        out.append(a * x[i - 1] + b * x[i] + c * x[i + 1] + d * x[i + 2])
    out.append(a * x[5] + b * x[6] + cd * x[7])
    out.append(a * x[6] + bcd * x[7])
    wx = place_weights(wx, column, 7)
    wz = place_weights(wz, level, LEV - 1)
    done = []
    for v in out:
        v = (
            wx[0] * pltpu.roll(v, 1, 0)
            + wx[1] * v
            + wx[2] * pltpu.roll(v, 7, 0)
            + wx[3] * pltpu.roll(v, 6, 0)
        )
        v = (
            wz[0] * pltpu.roll(v, step, 1)
            + wz[1] * v
            + wz[2] * pltpu.roll(v, values - step, 1)
            + wz[3] * pltpu.roll(v, values - 2 * step, 1)
        )
        done.append(v)
    return done


def quotient(x, n):
    if n & (n - 1) == 0:
        return lax.shift_right_logical(x, jnp.full_like(x, n.bit_length() - 1))
    return lax.div(x, jnp.full_like(x, n))


def make_tables(br, bc, lats, lat, lon, source, shift, near, near_shift, ti, tf):
    np_ = br * bc
    rows = br * 8
    lat_rows, total_cols = source.shape[1:]
    lanes = ti.shape[1]
    lane = lax.broadcasted_iota(jnp.int32, (8, lanes), 1)
    sub = lax.broadcasted_iota(jnp.int32, (8, lanes), 0)
    at = lax.broadcasted_iota(jnp.int32, (total_cols, lanes), 0)
    entry = lax.broadcasted_iota(jnp.int32, (total_cols, lanes), 1)
    pick_columns = jnp.where(at == lon * bc + entry % bc, 1.0, 0.0)
    near[...] = jnp.dot(
        source[...].reshape(STEPS * lat_rows, total_cols).astype(jnp.float32),
        pick_columns,
        precision=lax.Precision.HIGHEST,
        preferred_element_type=jnp.float32,
    )
    near_shift[...] = jnp.dot(
        shift[...].reshape(STEPS * 3 * lat_rows, total_cols),
        pick_columns,
        precision=lax.Precision.HIGHEST,
        preferred_element_type=jnp.float32,
    )
    row_of = lax.broadcasted_iota(jnp.int32, (br, lanes), 1) // bc
    own_row = row_of == lax.broadcasted_iota(jnp.int32, (br, lanes), 0)

    def band(ref, first):
        block = ref[pl.ds(first, br), :]
        return jnp.sum(jnp.where(own_row, block, 0.0), axis=0, keepdims=True)

    parts = [band(near_shift, k * lat_rows + lat * br) for k in range(STEPS * 3)]
    parts += [parts[0]] * (8 - STEPS * 3)
    for k, w in enumerate(cubic_weights(jnp.concatenate(parts, axis=0))):
        tf[8 * k : 8 * k + 8, :] = w
    latitude = ((lat * rows + lane).astype(jnp.float32) + 0.5) * (
        math.pi / (rows * lats)
    ) - 0.5 * math.pi
    tf[32:40, :] = jnp.cos(latitude)

    valid = lane < np_
    dest = jnp.clip(lat + jnp.minimum(sub, 4) - 2, 0, lats - 1)
    own_rows = []
    for s in range(STEPS):
        places = [
            s * lat_rows + jnp.clip(lat + o, 0, lats - 1) * br for o in range(-2, 3)
        ]
        bands = [band(near, p) for p in places]
        bands += [bands[4]] * 3
        ids = jnp.concatenate(bands, axis=0).astype(jnp.int32)
        source_row = quotient(ids, total_cols)
        source_dev = quotient(source_row, br)
        source_q = (ids - source_row * total_cols - lon * bc) * br + (
            source_row - source_dev * br
        )
        relative = source_dev - dest + 2
        count = jnp.zeros((8, lanes), jnp.int32)
        for k in range(5):
            count = jnp.where((relative == k) & valid, 1 << (6 * k), count)
        reach = 1
        while reach < np_:
            count = count + jnp.where(lane >= reach, pltpu.roll(count, reach, 1), 0)
            reach *= 2
        rank = jnp.zeros((8, lanes), jnp.int32)
        for k in range(5):
            field = lax.shift_right_logical(count, jnp.full_like(count, 6 * k))
            rank = jnp.where(relative == k, (field & 63) - 1, rank)
        code = jnp.where((source_dev == lat) & valid, rank, -1)

        def spread(x, picks):
            return jnp.concatenate(
                [jnp.broadcast_to(x[p : p + 1], (CAP, lanes)) for p in picks], axis=0
            )

        outer = (0, 1, 3, 4)
        slot = lax.broadcasted_iota(jnp.int32, (4 * CAP, lanes), 0)
        which = slot // CAP
        which = jnp.where(which >= 2, which + 1, which)
        slot = slot % CAP
        place = lax.broadcasted_iota(jnp.int32, (4 * CAP, lanes), 1)
        sent = jnp.where(spread(code, outer) == slot, spread(source_q, outer), 0)
        mine = (2,) * 4
        hit = (spread(relative, mine) == which) & (spread(rank, mine) == slot)
        come = jnp.where(hit & (place < np_), place, 0)
        sent = jnp.sum(sent.astype(jnp.float32), axis=1, keepdims=True)
        if s == 0:
            first_sent = jnp.clip(sent.astype(jnp.int32), 0, np_ - 1)
        come = jnp.sum(come.astype(jnp.float32), axis=1, keepdims=True)
        ti[s * 4 * CAP : (s + 1) * 4 * CAP, :] = jnp.clip(
            jnp.where(place == 0, sent, come).astype(jnp.int32), 0, np_ - 1
        )
        here = relative == 2
        outer_place = jnp.where(relative > 2, relative - 1, relative) * CAP + rank
        own_rows.append(jnp.clip(jnp.where(here & valid, source_q, 0), 0, np_ - 1)[2:3])
        outer_place = jnp.clip(outer_place, 0, 4 * CAP - 1)
        own_rows.append(jnp.where(here | ~valid, -1, outer_place)[2:3])
    own_rows += own_rows[:1] * (8 - len(own_rows))
    ti[STEPS * 4 * CAP :, :] = jnp.concatenate(own_rows, axis=0)
    return first_sent


def several(count, unroll, body, carry):
    def turn(i, carry):
        for k in range(unroll):
            carry = body(i * unroll + k, carry)
        return carry

    return lax.fori_loop(0, count // unroll, turn, carry)


def kernel(
    br, bc, lats, lons,
    source_hbm, shift_hbm, kappa_hbm, tr, out,
    st, arr, ia, snd, adv, row_in, side_out, side_in, ka_out, ka_in, mass_out, mass_in,
    source, shift, near, near_shift, ti_v, tf_v, ti, tf, kappa, weight,
    load_sem, small_sem, psend, precv, hsend, hrecv, ksend, krecv, msend, mrecv,
):
    np_ = br * bc
    rows = br * 8
    peers = lats * lons
    values = tr.shape[-1]
    lat = lax.axis_index("lat")
    lon = lax.axis_index("lon")

    small = [
        pltpu.make_async_copy(source_hbm, source, small_sem.at[0]),
        pltpu.make_async_copy(shift_hbm, shift, small_sem.at[1]),
        pltpu.make_async_copy(kappa_hbm, kappa, small_sem.at[2]),
    ]
    for copy in small:
        copy.start()
    loads = [
        pltpu.make_async_copy(
            tr.at[:, :, c], st.at[0, pl.ds(c * br, br)], load_sem.at[c]
        )
        for c in range(bc)
    ]
    for copy in loads:
        copy.start()

    zero = jnp.zeros((8, values), jnp.float32)
    for s in range(STEPS):
        for c in range(bc):
            adv[s, c, 0] = zero
            adv[s, c, rows + 1] = zero
    ka_in[...] = jnp.zeros_like(ka_in)
    row_in[...] = jnp.zeros_like(row_in)

    def peer(k):
        return {
            "lat": lax.rem(lat + k // lons, lats),
            "lon": lax.rem(lon + lax.rem(k, lons), lons),
        }

    barrier = pltpu.get_barrier_semaphore()

    def greet(k, _):
        pl.semaphore_signal(barrier, inc=1, device_id=peer(k), device_id_type=MESH)
        return 0

    lax.fori_loop(1, peers, greet, 0)
    for copy in small:
        copy.wait()
    first_sent = make_tables(
        br, bc, lats, lat, lon, source, shift, near, near_shift, ti_v, tf_v
    )
    to_scalar = [
        pltpu.make_async_copy(ti_v, ti, small_sem.at[3]),
        pltpu.make_async_copy(tf_v, tf, small_sem.at[4]),
    ]
    for copy in to_scalar:
        copy.start()
    pl.semaphore_wait(barrier, peers - 1)

    def in_range(offset):
        return (lat + offset >= 0) & (lat + offset < lats)

    def patch_copy(s, o, h):
        return pltpu.make_async_remote_copy(
            src_ref=snd.at[s, o, pl.ds(h * PIECE, PIECE)],
            dst_ref=arr.at[s, 3 - o, pl.ds(h * PIECE, PIECE)],
            send_sem=psend.at[s, o, h],
            recv_sem=precv.at[s, 3 - o, h],
            device_id={"lat": jnp.clip(lat + OFFSETS[o], 0, lats - 1), "lon": lon},
            device_id_type=MESH,
        )

    def ka_copy(i):
        return pltpu.make_async_remote_copy(
            src_ref=ka_out.at[i],
            dst_ref=ka_in.at[1 - i],
            send_sem=ksend.at[i],
            recv_sem=krecv.at[1 - i],
            device_id={"lat": jnp.clip(lat + 2 * i - 1, 0, lats - 1), "lon": lon},
            device_id_type=MESH,
        )

    def row_copy(s, i):
        return pltpu.make_async_remote_copy(
            src_ref=adv.at[s, :, rows if i else 1],
            dst_ref=row_in.at[s, 1 - i],
            send_sem=hsend.at[s, i],
            recv_sem=hrecv.at[s, 1 - i],
            device_id={"lat": jnp.clip(lat + 2 * i - 1, 0, lats - 1), "lon": lon},
            device_id_type=MESH,
        )

    def column_copy(s, i):
        return pltpu.make_async_remote_copy(
            src_ref=side_out.at[s, i],
            dst_ref=side_in.at[s, 1 - i],
            send_sem=hsend.at[s, 2 + i],
            recv_sem=hrecv.at[s, 3 - i],
            device_id={"lat": lat, "lon": lax.rem(lon + lons + 2 * i - 1, lons)},
            device_id_type=MESH,
        )

    def send_patches(s, index):
        for o in SENT_FIRST:
            for h in range(PIECES):
                for j in range(h * PIECE, (h + 1) * PIECE):
                    snd[s, o, j] = st[s, index[o * CAP + j]]

                @pl.when(in_range(OFFSETS[o]))
                def _():
                    patch_copy(s, o, h).start()

    def weights(s, e):
        return [[tf[8 * k + s * 3 + i, e] for k in range(4)] for i in range(3)]

    def masses(s):
        def send(k, _):
            pltpu.make_async_remote_copy(
                src_ref=mass_out.at[s],
                dst_ref=mass_in.at[s, k],
                send_sem=msend.at[s],
                recv_sem=mrecv.at[s],
                device_id=peer(k),
                device_id_type=MESH,
            ).start()
            return 0

        lax.fori_loop(1, peers, send, 0)

    def masses_sum(s):
        others = mass_in.at[s, pl.ds(1, peers - 1)]
        pltpu.make_async_copy(others, others, mrecv.at[s]).wait()
        return jnp.sum(mass_in[s], axis=0)

    def advect(s, ratio):
        def own(q, _):
            c, r = q // br, lax.rem(q, br)
            e = r * bc + c
            block = st[s, ti[STEPS * 4 * CAP + 2 * s, e]]
            done = interpolate([block[i] for i in range(8)], weights(s, e), ratio)
            for i in range(8):
                adv[s, c, 1 + r * 8 + i] = done[i]
            return 0

        several(np_, 4, own, 0)
        odd = lax.rem(lat, 2)

        def arrivals(t, _):
            turn, h = t // PIECES, lax.rem(t, PIECES)
            o = jnp.where(turn == 0, 2 - odd, jnp.where(turn == 3, 1 + odd, 3 * (turn - 1)))
            offset = o - 2 + jnp.where(o >= 2, 1, 0)

            @pl.when(in_range(offset))
            def _():
                piece = arr.at[s, o, pl.ds(h * PIECE, PIECE)]
                pltpu.make_async_copy(piece, piece, precv.at[s, o, h]).wait()
                for k in range(PIECE):
                    j = h * PIECE + k
                    e = ti[(s * 4 + o) * CAP + j, 1]
                    block = arr[s, o, j]
                    done = interpolate(
                        [block[i] for i in range(8)], weights(s, e), ratio
                    )
                    for i in range(8):
                        ia[s, o * CAP + j, i] = done[i]

            return 0

        lax.fori_loop(0, 4 * PIECES, arrivals, 0)

        def join(q, total):
            c, r = q // br, lax.rem(q, br)
            e = r * bc + c
            pick = ti[STEPS * 4 * CAP + 2 * s + 1, e]
            block = ia[s, jnp.maximum(pick, 0)]
            far = jnp.full((8, values), pick, jnp.int32) >= 0
            for i in range(8):
                v = jnp.where(far, block[i], adv[s, c, 1 + r * 8 + i])
                adv[s, c, 1 + r * 8 + i] = v
                total = total + weight[r * 8 + i] * v
            return total

        total = several(np_, 4, join, zero)
        for i in range(2):

            @pl.when(in_range(2 * i - 1))
            def _():
                row_copy(s, i).start()

        for i in range(rows):
            side_out[s, 0, i : i + 1] = adv[s, 0, 1 + i][0:1]
            side_out[s, 1, i : i + 1] = adv[s, bc - 1, 1 + i][7:8]
        for i in range(2):
            column_copy(s, i).start()
        first = functools.reduce(jnp.add, [adv[s, c, 1] for c in range(bc)])
        last = functools.reduce(jnp.add, [adv[s, c, rows] for c in range(bc)])
        return total + first * ka_in[0] + last * ka_in[1]

    def wait_halos(s):
        for i in range(2):

            @pl.when(in_range(2 * i - 1))
            def _():
                row_copy(s, 1 - i).wait_recv()

            column_copy(s, 1 - i).wait_recv()

    column = lax.broadcasted_iota(jnp.int32, (8, values), 0)

    def add_halos(s, place):
        ref, where = place
        for i, row in enumerate((0, rows - 1)):
            for c in range(bc):
                at = where(row, c)
                ref[at] = ref[at] + kappa[row] * row_in[s, i, c]

        def sides(row, _):
            for i, c in enumerate((0, bc - 1)):
                at = where(row, c)
                side = jnp.broadcast_to(side_in[s, i, pl.ds(row, 1)], (8, values))
                side = jnp.where(column == (7 if i else 0), side, 0.0)
                ref[at] = ref[at] + kappa[row] * side
            return 0

        several(rows, 8, sides, 0)

    def diffused_row(s, row):
        here = [adv[s, c, 1 + row] for c in range(bc)]
        ahead = [pltpu.roll(v, 7, 0) for v in here]
        behind = [pltpu.roll(v, 1, 0) for v in here]
        number = kappa[row]
        result = []
        for c in range(bc):
            e = jnp.where(column == 7, 0.0 if c == bc - 1 else ahead[c + 1], ahead[c])
            w = jnp.where(column == 0, 0.0 if c == 0 else behind[c - 1], behind[c])
            lap = adv[s, c, row] + adv[s, c, row + 2] + e + w - 4.0 * here[c]
            result.append(here[c] + number * lap)
        return result

    for copy in loads:
        copy.wait()
    send_patches(0, [first_sent[k, 0] for k in range(4 * CAP)])
    for copy in to_scalar:
        copy.wait()

    def area(row):
        return tf[32, row]

    for i, row in enumerate((0, rows - 1)):
        ka_out[i] = jnp.full((1, values), kappa[row] * area(row), jnp.float32)
    for i in range(2):

        @pl.when(in_range(2 * i - 1))
        def _():
            ka_copy(i).start()


    for row in range(rows):
        w = area(row) * (1.0 - 2.0 * kappa[row])
        if row:
            w = w + area(row - 1) * kappa[row - 1]
        if row < rows - 1:
            w = w + area(row + 1) * kappa[row + 1]
        weight[row] = w

    def target_row(row, total):
        parts = [st[0, c * br + row // 8, lax.rem(row, 8)] for c in range(bc)]
        return total + area(row) * functools.reduce(jnp.add, parts)

    target_part = several(rows, 4, target_row, zero)
    for i in range(2):

        @pl.when(in_range(2 * i - 1))
        def _():
            ka_copy(1 - i).wait_recv()

    total = advect(0, None)
    both = jnp.concatenate(
        [
            jnp.sum(total, axis=0, keepdims=True),
            jnp.sum(target_part, axis=0, keepdims=True),
        ],
        axis=0,
    )
    mass_out[0] = both
    mass_in[0, 0] = both
    masses(0)

    def in_state(row, c):
        return 1, c * br + row // 8, row % 8 if isinstance(row, int) else lax.rem(row, 8)

    def first_step(row, _):
        done = diffused_row(0, row)
        for c in range(bc):
            st[in_state(row, c)] = done[c]
        return 0

    several(rows, 4, first_step, 0)
    wait_halos(0)
    add_halos(0, (st, in_state))
    send_patches(1, [ti[4 * CAP + k, 0] for k in range(4 * CAP)])
    sums = masses_sum(0)
    target = sums[1:2]
    ratio = jnp.broadcast_to(target / sums[0:1], (8, values))
    total = advect(1, ratio)
    both = jnp.broadcast_to(jnp.sum(total, axis=0, keepdims=True), (2, values))
    mass_out[1] = both
    mass_in[1, 0] = both
    masses(1)

    def in_out(row, c):
        return row // 8, row % 8 if isinstance(row, int) else lax.rem(row, 8), c

    def last_step(row, _):
        done = diffused_row(1, row)
        for c in range(bc):
            out[in_out(row, c)] = done[c]
        return 0

    several(rows, 4, last_step, 0)
    wait_halos(1)
    add_halos(1, (out, in_out))
    ratio = jnp.broadcast_to(target / masses_sum(1)[0:1], (8, values))

    def scale(row, _):
        for c in range(bc):
            out[in_out(row, c)] = out[in_out(row, c)] * ratio
        return 0

    several(rows, 4, scale, 0)

    for s in range(STEPS):
        for o in range(4):

            @pl.when(in_range(OFFSETS[o]))
            def _():
                for h in range(PIECES):
                    patch_copy(s, o, h).wait_send()

        for i in range(2):

            @pl.when(in_range(2 * i - 1))
            def _():
                row_copy(s, i).wait_send()

            column_copy(s, i).wait_send()
        others = mass_in.at[s, pl.ds(1, peers - 1)]
        pltpu.make_async_copy(others, others, msend.at[s]).wait()
    for i in range(2):

        @pl.when(in_range(2 * i - 1))
        def _():
            ka_copy(i).wait_send()


def local(lats, lons, tracers, shifts, diffusivity, source_patch):
    rows, cols, values = tracers.shape
    br, bc = rows // 8, cols // 8
    np_ = br * bc
    tile = (8, 8, values)
    peers = lats * lons
    dma = pltpu.SemaphoreType.DMA
    f32 = jnp.float32
    result = pl.pallas_call(
        functools.partial(kernel, br, bc, lats, lons),
        out_shape=pltpu.VMEM((br, 8, bc, 8, values), f32),
        in_specs=[
            pl.BlockSpec(memory_space=pltpu.HBM),
            pl.BlockSpec(memory_space=pltpu.HBM),
            pl.BlockSpec(memory_space=pltpu.HBM),
            pl.BlockSpec(memory_space=pltpu.HBM),
        ],
        out_specs=pl.BlockSpec(memory_space=pltpu.VMEM),
        scratch_shapes=[
            pltpu.VMEM((STEPS, np_) + tile, f32),
            pltpu.VMEM((STEPS, 4, CAP) + tile, f32),
            pltpu.VMEM((STEPS, 4 * CAP) + tile, f32),
            pltpu.VMEM((STEPS, 4, CAP) + tile, f32),
            pltpu.VMEM((STEPS, bc, rows + 2, 8, values), f32),
            pltpu.VMEM((STEPS, 2, bc, 8, values), f32),
            pltpu.VMEM((STEPS, 2, rows, values), f32),
            pltpu.VMEM((STEPS, 2, rows, values), f32),
            pltpu.VMEM((2, 1, values), f32),
            pltpu.VMEM((2, 1, values), f32),
            pltpu.VMEM((STEPS, 2, values), f32),
            pltpu.VMEM((STEPS, peers, 2, values), f32),
            pltpu.VMEM(source_patch.shape, jnp.int32),
            pltpu.VMEM(shifts.shape, f32),
            pltpu.VMEM((STEPS * source_patch.shape[1], 128), f32),
            pltpu.VMEM((STEPS * 3 * source_patch.shape[1], 128), f32),
            pltpu.VMEM((STEPS * 4 * CAP + 8, 128), jnp.int32),
            pltpu.VMEM((40, 128), f32),
            pltpu.SMEM((STEPS * 4 * CAP + 8, 128), jnp.int32),
            pltpu.SMEM((40, 128), f32),
            pltpu.SMEM((rows,), f32),
            pltpu.SMEM((rows,), f32),
            dma((bc,)),
            dma((5,)),
            dma((STEPS, 4, PIECES)),
            dma((STEPS, 4, PIECES)),
            dma((STEPS, 4)),
            dma((STEPS, 4)),
            dma((2,)),
            dma((2,)),
            dma((STEPS,)),
            dma((STEPS,)),
        ],
        compiler_params=pltpu.CompilerParams(
            collective_id=0, has_side_effects=True, vmem_limit_bytes=32 * 1024 * 1024
        ),
    )(
        *(
            pltpu.with_memory_space_constraint(x, pltpu.HBM)
            for x in (
                source_patch,
                shifts,
                diffusivity,
                tracers.reshape(br, 8, bc, 8, values),
            )
        )
    )
    return result.reshape(rows, cols, values)


def solution(mesh):
    return jax.shard_map(
        functools.partial(local, mesh.shape["lat"], mesh.shape["lon"]),
        mesh=mesh,
        in_specs=(
            P(("groups", "lat"), "lon", None),
            P("groups", None, None, None),
            P("lat"),
            P("groups", None, None),
        ),
        out_specs=P(("groups", "lat"), "lon", None),
        check_vma=False,
    )
```

```python
import functools
import math

import jax
import jax.numpy as jnp
from jax import lax
from jax.experimental import pallas as pl
from jax.experimental.pallas import tpu as pltpu
from jax.sharding import PartitionSpec as P

LEV = 4
STEPS = 2
CAP = 4
OFFSETS = (-2, -1, 1, 2)
SENT_FIRST = (0, 3, 1, 2)
PIECES = 1
PIECE = CAP // PIECES
MESH = pl.DeviceIdType.MESH


def cubic_weights(s):
    return (
        -s * (s - 1.0) * (s - 2.0) * (1.0 / 6.0),
        (s + 1.0) * (s - 1.0) * (s - 2.0) * 0.5,
        -(s + 1.0) * s * (s - 2.0) * 0.5,
        (s + 1.0) * s * (s - 1.0) * (1.0 / 6.0),
    )


def place_weights(w, place, last):
    a, b, c, d = w
    return (
        jnp.where(place == 0, 0.0, a),
        b + jnp.where(place == 0, a, 0.0) + jnp.where(place == last, c + d, 0.0),
        jnp.where(place == last, 0.0, c + jnp.where(place == last - 1, d, 0.0)),
        jnp.where(place >= last - 1, 0.0, d),
    )


def interpolate(rows, weights, ratio):
    values = rows[0].shape[1]
    step = values // LEV
    column = lax.broadcasted_iota(jnp.int32, (8, values), 0)
    level = lax.broadcasted_iota(jnp.int32, (8, values), 1) // step
    wy, wx, wz = (
        [jnp.full((8, values), w, jnp.float32) for w in part] for part in weights
    )
    a, b, c, d = wy
    ab, cd = a + b, c + d
    bcd = b + cd
    x = rows
    if ratio is not None:
        x = [r * ratio for r in x]
    out = [ab * x[0] + c * x[1] + d * x[2]]
    for i in range(1, 6):
        out.append(a * x[i - 1] + b * x[i] + c * x[i + 1] + d * x[i + 2])
    out.append(a * x[5] + b * x[6] + cd * x[7])
    out.append(a * x[6] + bcd * x[7])
    wx = place_weights(wx, column, 7)
    wz = place_weights(wz, level, LEV - 1)
    done = []
    for v in out:
        v = (
            wx[0] * pltpu.roll(v, 1, 0)
            + wx[1] * v
            + wx[2] * pltpu.roll(v, 7, 0)
            + wx[3] * pltpu.roll(v, 6, 0)
        )
        v = (
            wz[0] * pltpu.roll(v, step, 1)
            + wz[1] * v
            + wz[2] * pltpu.roll(v, values - step, 1)
            + wz[3] * pltpu.roll(v, values - 2 * step, 1)
        )
        done.append(v)
    return done


def quotient(x, n):
    if n & (n - 1) == 0:
        return lax.shift_right_logical(x, jnp.full_like(x, n.bit_length() - 1))
    return lax.div(x, jnp.full_like(x, n))


def make_tables(br, bc, lats, lat, lon, source, shift, near, near_shift, ti, tf):
    np_ = br * bc
    rows = br * 8
    lat_rows, total_cols = source.shape[1:]
    lanes = ti.shape[1]
    lane = lax.broadcasted_iota(jnp.int32, (8, lanes), 1)
    sub = lax.broadcasted_iota(jnp.int32, (8, lanes), 0)
    at = lax.broadcasted_iota(jnp.int32, (total_cols, lanes), 0)
    entry = lax.broadcasted_iota(jnp.int32, (total_cols, lanes), 1)
    pick_columns = jnp.where(at == lon * bc + entry % bc, 1.0, 0.0)
    near[...] = jnp.dot(
        source[...].reshape(STEPS * lat_rows, total_cols).astype(jnp.float32),
        pick_columns,
        precision=lax.Precision.HIGHEST,
        preferred_element_type=jnp.float32,
    )
    near_shift[...] = jnp.dot(
        shift[...].reshape(STEPS * 3 * lat_rows, total_cols),
        pick_columns,
        precision=lax.Precision.HIGHEST,
        preferred_element_type=jnp.float32,
    )
    row_of = lax.broadcasted_iota(jnp.int32, (br, lanes), 1) // bc
    own_row = row_of == lax.broadcasted_iota(jnp.int32, (br, lanes), 0)

    def band(ref, first):
        block = ref[pl.ds(first, br), :]
        return jnp.sum(jnp.where(own_row, block, 0.0), axis=0, keepdims=True)

    parts = [band(near_shift, k * lat_rows + lat * br) for k in range(STEPS * 3)]
    parts += [parts[0]] * (8 - STEPS * 3)
    for k, w in enumerate(cubic_weights(jnp.concatenate(parts, axis=0))):
        tf[8 * k : 8 * k + 8, :] = w
    latitude = ((lat * rows + lane).astype(jnp.float32) + 0.5) * (
        math.pi / (rows * lats)
    ) - 0.5 * math.pi
    tf[32:40, :] = jnp.cos(latitude)

    valid = lane < np_
    dest = jnp.clip(lat + jnp.minimum(sub, 4) - 2, 0, lats - 1)
    own_rows = []
    for s in range(STEPS):
        places = [
            s * lat_rows + jnp.clip(lat + o, 0, lats - 1) * br for o in range(-2, 3)
        ]
        bands = [band(near, p) for p in places]
        bands += [bands[4]] * 3
        ids = jnp.concatenate(bands, axis=0).astype(jnp.int32)
        source_row = quotient(ids, total_cols)
        source_dev = quotient(source_row, br)
        source_q = (ids - source_row * total_cols - lon * bc) * br + (
            source_row - source_dev * br
        )
        relative = source_dev - dest + 2
        count = jnp.zeros((8, lanes), jnp.int32)
        for k in range(5):
            count = jnp.where((relative == k) & valid, 1 << (6 * k), count)
        reach = 1
        while reach < np_:
            count = count + jnp.where(lane >= reach, pltpu.roll(count, reach, 1), 0)
            reach *= 2
        rank = jnp.zeros((8, lanes), jnp.int32)
        for k in range(5):
            field = lax.shift_right_logical(count, jnp.full_like(count, 6 * k))
            rank = jnp.where(relative == k, (field & 63) - 1, rank)
        code = jnp.where((source_dev == lat) & valid, rank, -1)

        def spread(x, picks):
            return jnp.concatenate(
                [jnp.broadcast_to(x[p : p + 1], (CAP, lanes)) for p in picks], axis=0
            )

        outer = (0, 1, 3, 4)
        slot = lax.broadcasted_iota(jnp.int32, (4 * CAP, lanes), 0)
        which = slot // CAP
        which = jnp.where(which >= 2, which + 1, which)
        slot = slot % CAP
        place = lax.broadcasted_iota(jnp.int32, (4 * CAP, lanes), 1)
        sent = jnp.where(spread(code, outer) == slot, spread(source_q, outer), 0)
        mine = (2,) * 4
        hit = (spread(relative, mine) == which) & (spread(rank, mine) == slot)
        come = jnp.where(hit & (place < np_), place, 0)
        sent = jnp.sum(sent.astype(jnp.float32), axis=1, keepdims=True)
        if s == 0:
            first_sent = jnp.clip(sent.astype(jnp.int32), 0, np_ - 1)
        come = jnp.sum(come.astype(jnp.float32), axis=1, keepdims=True)
        ti[s * 4 * CAP : (s + 1) * 4 * CAP, :] = jnp.clip(
            jnp.where(place == 0, sent, come).astype(jnp.int32), 0, np_ - 1
        )
        here = relative == 2
        outer_place = jnp.where(relative > 2, relative - 1, relative) * CAP + rank
        own_rows.append(jnp.clip(jnp.where(here & valid, source_q, 0), 0, np_ - 1)[2:3])
        outer_place = jnp.clip(outer_place, 0, 4 * CAP - 1)
        own_rows.append(jnp.where(here | ~valid, -1, outer_place)[2:3])
    own_rows += own_rows[:1] * (8 - len(own_rows))
    ti[STEPS * 4 * CAP :, :] = jnp.concatenate(own_rows, axis=0)
    return first_sent


def several(count, unroll, body, carry):
    def turn(i, carry):
        for k in range(unroll):
            carry = body(i * unroll + k, carry)
        return carry

    return lax.fori_loop(0, count // unroll, turn, carry)


def kernel(
    br, bc, lats, lons,
    source_hbm, shift_hbm, kappa_hbm, tr, out,
    st, arr, ia, snd, adv, row_in, side_out, side_in, ka_out, ka_in, mass_out, mass_in,
    source, shift, near, near_shift, ti_v, tf_v, ti, tf, kappa, weight,
    load_sem, small_sem, psend, precv, hsend, hrecv, ksend, krecv, msend, mrecv,
):
    np_ = br * bc
    rows = br * 8
    peers = lats * lons
    values = tr.shape[-1]
    lat = lax.axis_index("lat")
    lon = lax.axis_index("lon")

    small = [
        pltpu.make_async_copy(source_hbm, source, small_sem.at[0]),
        pltpu.make_async_copy(shift_hbm, shift, small_sem.at[1]),
        pltpu.make_async_copy(kappa_hbm, kappa, small_sem.at[2]),
    ]
    for copy in small:
        copy.start()
    loads = [
        pltpu.make_async_copy(
            tr.at[:, :, c], st.at[0, pl.ds(c * br, br)], load_sem.at[c]
        )
        for c in range(bc)
    ]
    for copy in loads:
        copy.start()

    zero = jnp.zeros((8, values), jnp.float32)
    for s in range(STEPS):
        for c in range(bc):
            adv[s, c, 0] = zero
            adv[s, c, rows + 1] = zero
    ka_in[...] = jnp.zeros_like(ka_in)
    row_in[...] = jnp.zeros_like(row_in)

    def peer(k):
        return {
            "lat": lax.rem(lat + k // lons, lats),
            "lon": lax.rem(lon + lax.rem(k, lons), lons),
        }

    barrier = pltpu.get_barrier_semaphore()

    def greet(k, _):
        pl.semaphore_signal(barrier, inc=1, device_id=peer(k), device_id_type=MESH)
        return 0

    lax.fori_loop(1, peers, greet, 0)
    for copy in small:
        copy.wait()
    first_sent = make_tables(
        br, bc, lats, lat, lon, source, shift, near, near_shift, ti_v, tf_v
    )
    to_scalar = [
        pltpu.make_async_copy(ti_v, ti, small_sem.at[3]),
        pltpu.make_async_copy(tf_v, tf, small_sem.at[4]),
    ]
    for copy in to_scalar:
        copy.start()
    pl.semaphore_wait(barrier, peers - 1)

    def in_range(offset):
        return (lat + offset >= 0) & (lat + offset < lats)

    def patch_copy(s, o, h):
        return pltpu.make_async_remote_copy(
            src_ref=snd.at[s, o, pl.ds(h * PIECE, PIECE)],
            dst_ref=arr.at[s, 3 - o, pl.ds(h * PIECE, PIECE)],
            send_sem=psend.at[s, o, h],
            recv_sem=precv.at[s, 3 - o, h],
            device_id={"lat": jnp.clip(lat + OFFSETS[o], 0, lats - 1), "lon": lon},
            device_id_type=MESH,
        )

    def ka_copy(i):
        return pltpu.make_async_remote_copy(
            src_ref=ka_out.at[i],
            dst_ref=ka_in.at[1 - i],
            send_sem=ksend.at[i],
            recv_sem=krecv.at[1 - i],
            device_id={"lat": jnp.clip(lat + 2 * i - 1, 0, lats - 1), "lon": lon},
            device_id_type=MESH,
        )

    def row_copy(s, i):
        return pltpu.make_async_remote_copy(
            src_ref=adv.at[s, :, rows if i else 1],
            dst_ref=row_in.at[s, 1 - i],
            send_sem=hsend.at[s, i],
            recv_sem=hrecv.at[s, 1 - i],
            device_id={"lat": jnp.clip(lat + 2 * i - 1, 0, lats - 1), "lon": lon},
            device_id_type=MESH,
        )

    def column_copy(s, i):
        return pltpu.make_async_remote_copy(
            src_ref=side_out.at[s, i],
            dst_ref=side_in.at[s, 1 - i],
            send_sem=hsend.at[s, 2 + i],
            recv_sem=hrecv.at[s, 3 - i],
            device_id={"lat": lat, "lon": lax.rem(lon + lons + 2 * i - 1, lons)},
            device_id_type=MESH,
        )

    def send_patches(s, index):
        for o in SENT_FIRST:
            for h in range(PIECES):
                for j in range(h * PIECE, (h + 1) * PIECE):
                    snd[s, o, j] = st[s, index[o * CAP + j]]

                @pl.when(in_range(OFFSETS[o]))
                def _():
                    patch_copy(s, o, h).start()

    def weights(s, e):
        return [[tf[8 * k + s * 3 + i, e] for k in range(4)] for i in range(3)]

    def masses(s):
        def send(k, _):
            pltpu.make_async_remote_copy(
                src_ref=mass_out.at[s],
                dst_ref=mass_in.at[s, k],
                send_sem=msend.at[s],
                recv_sem=mrecv.at[s],
                device_id=peer(k),
                device_id_type=MESH,
            ).start()
            return 0

        lax.fori_loop(1, peers, send, 0)

    def masses_sum(s):
        others = mass_in.at[s, pl.ds(1, peers - 1)]
        pltpu.make_async_copy(others, others, mrecv.at[s]).wait()
        return jnp.sum(mass_in[s], axis=0)

    def advect(s, ratio):
        def own(q, _):
            c, r = q // br, lax.rem(q, br)
            e = r * bc + c
            block = st[s, ti[STEPS * 4 * CAP + 2 * s, e]]
            done = interpolate([block[i] for i in range(8)], weights(s, e), ratio)
            for i in range(8):
                adv[s, c, 1 + r * 8 + i] = done[i]
            return 0

        several(np_, 8, own, 0)
        odd = lax.rem(lat, 2)

        def come(o, j):
            e = ti[(s * 4 + o) * CAP + j, 1]
            block = arr[s, o, j]
            done = interpolate([block[i] for i in range(8)], weights(s, e), ratio)
            for i in range(8):
                ia[s, o * CAP + j, i] = done[i]

        def arrived(o):
            offset = o - 2 + jnp.where(o >= 2, 1, 0)

            @pl.when(in_range(offset))
            def _():
                piece = arr.at[s, o]
                pltpu.make_async_copy(piece, piece, precv.at[s, o, 0]).wait()

        arrived(2 - odd)
        for j in range(CAP):
            come(2 - odd, j)
        far = (0, 3, 1 + odd)
        for o in far:
            arrived(o)
        for o in far:
            for j in range(CAP):
                come(o, j)

        def join(q, total):
            c, r = q // br, lax.rem(q, br)
            e = r * bc + c
            pick = ti[STEPS * 4 * CAP + 2 * s + 1, e]
            block = ia[s, jnp.maximum(pick, 0)]
            far = jnp.full((8, values), pick, jnp.int32) >= 0
            for i in range(8):
                v = jnp.where(far, block[i], adv[s, c, 1 + r * 8 + i])
                adv[s, c, 1 + r * 8 + i] = v
                total = total + weight[r * 8 + i] * v
            return total

        total = several(np_, 8, join, zero)
        for i in range(2):

            @pl.when(in_range(2 * i - 1))
            def _():
                row_copy(s, i).start()

        for i in range(rows):
            side_out[s, 0, i : i + 1] = adv[s, 0, 1 + i][0:1]
            side_out[s, 1, i : i + 1] = adv[s, bc - 1, 1 + i][7:8]
        for i in range(2):
            column_copy(s, i).start()
        first = functools.reduce(jnp.add, [adv[s, c, 1] for c in range(bc)])
        last = functools.reduce(jnp.add, [adv[s, c, rows] for c in range(bc)])
        return total + first * ka_in[0] + last * ka_in[1]

    def wait_halos(s):
        for i in range(2):

            @pl.when(in_range(2 * i - 1))
            def _():
                row_copy(s, 1 - i).wait_recv()

            column_copy(s, 1 - i).wait_recv()

    column = lax.broadcasted_iota(jnp.int32, (8, values), 0)

    def add_halos(s, place):
        ref, where = place
        for i, row in enumerate((0, rows - 1)):
            for c in range(bc):
                at = where(row, c)
                ref[at] = ref[at] + kappa[row] * row_in[s, i, c]

        def sides(row, _):
            for i, c in enumerate((0, bc - 1)):
                at = where(row, c)
                side = jnp.broadcast_to(side_in[s, i, pl.ds(row, 1)], (8, values))
                side = jnp.where(column == (7 if i else 0), side, 0.0)
                ref[at] = ref[at] + kappa[row] * side
            return 0

        several(rows, 8, sides, 0)

    def diffused_row(s, row):
        here = [adv[s, c, 1 + row] for c in range(bc)]
        ahead = [pltpu.roll(v, 7, 0) for v in here]
        behind = [pltpu.roll(v, 1, 0) for v in here]
        number = kappa[row]
        result = []
        for c in range(bc):
            e = jnp.where(column == 7, 0.0 if c == bc - 1 else ahead[c + 1], ahead[c])
            w = jnp.where(column == 0, 0.0 if c == 0 else behind[c - 1], behind[c])
            lap = adv[s, c, row] + adv[s, c, row + 2] + e + w - 4.0 * here[c]
            result.append(here[c] + number * lap)
        return result

    for copy in loads:
        copy.wait()
    send_patches(0, [first_sent[k, 0] for k in range(4 * CAP)])
    for copy in to_scalar:
        copy.wait()

    def area(row):
        return tf[32, row]

    for i, row in enumerate((0, rows - 1)):
        ka_out[i] = jnp.full((1, values), kappa[row] * area(row), jnp.float32)
    for i in range(2):

        @pl.when(in_range(2 * i - 1))
        def _():
            ka_copy(i).start()


    for row in range(rows):
        w = area(row) * (1.0 - 2.0 * kappa[row])
        if row:
            w = w + area(row - 1) * kappa[row - 1]
        if row < rows - 1:
            w = w + area(row + 1) * kappa[row + 1]
        weight[row] = w

    def target_row(row, total):
        parts = [st[0, c * br + row // 8, lax.rem(row, 8)] for c in range(bc)]
        return total + area(row) * functools.reduce(jnp.add, parts)

    target_part = several(rows, 4, target_row, zero)
    for i in range(2):

        @pl.when(in_range(2 * i - 1))
        def _():
            ka_copy(1 - i).wait_recv()

    total = advect(0, None)
    both = jnp.concatenate(
        [
            jnp.sum(total, axis=0, keepdims=True),
            jnp.sum(target_part, axis=0, keepdims=True),
        ],
        axis=0,
    )
    mass_out[0] = both
    mass_in[0, 0] = both
    masses(0)

    def in_state(row, c):
        return 1, c * br + row // 8, row % 8 if isinstance(row, int) else lax.rem(row, 8)

    def first_step(row, _):
        done = diffused_row(0, row)
        for c in range(bc):
            st[in_state(row, c)] = done[c]
        return 0

    several(rows, 8, first_step, 0)
    wait_halos(0)
    add_halos(0, (st, in_state))
    send_patches(1, [ti[4 * CAP + k, 0] for k in range(4 * CAP)])
    sums = masses_sum(0)
    target = sums[1:2]
    ratio = jnp.broadcast_to(target / sums[0:1], (8, values))
    total = advect(1, ratio)
    both = jnp.broadcast_to(jnp.sum(total, axis=0, keepdims=True), (2, values))
    mass_out[1] = both
    mass_in[1, 0] = both
    masses(1)

    def in_out(row, c):
        return row // 8, row % 8 if isinstance(row, int) else lax.rem(row, 8), c

    def last_step(row, _):
        done = diffused_row(1, row)
        for c in range(bc):
            out[in_out(row, c)] = done[c]
        return 0

    several(rows, 8, last_step, 0)
    wait_halos(1)
    add_halos(1, (out, in_out))
    ratio = jnp.broadcast_to(target / masses_sum(1)[0:1], (8, values))

    def scale(row, _):
        for c in range(bc):
            out[in_out(row, c)] = out[in_out(row, c)] * ratio
        return 0

    several(rows, 8, scale, 0)

    for s in range(STEPS):
        for o in range(4):

            @pl.when(in_range(OFFSETS[o]))
            def _():
                for h in range(PIECES):
                    patch_copy(s, o, h).wait_send()

        for i in range(2):

            @pl.when(in_range(2 * i - 1))
            def _():
                row_copy(s, i).wait_send()

            column_copy(s, i).wait_send()
        others = mass_in.at[s, pl.ds(1, peers - 1)]
        pltpu.make_async_copy(others, others, msend.at[s]).wait()
    for i in range(2):

        @pl.when(in_range(2 * i - 1))
        def _():
            ka_copy(i).wait_send()


def local(lats, lons, tracers, shifts, diffusivity, source_patch):
    rows, cols, values = tracers.shape
    br, bc = rows // 8, cols // 8
    np_ = br * bc
    tile = (8, 8, values)
    peers = lats * lons
    dma = pltpu.SemaphoreType.DMA
    f32 = jnp.float32
    result = pl.pallas_call(
        functools.partial(kernel, br, bc, lats, lons),
        out_shape=pltpu.VMEM((br, 8, bc, 8, values), f32),
        in_specs=[
            pl.BlockSpec(memory_space=pltpu.HBM),
            pl.BlockSpec(memory_space=pltpu.HBM),
            pl.BlockSpec(memory_space=pltpu.HBM),
            pl.BlockSpec(memory_space=pltpu.HBM),
        ],
        out_specs=pl.BlockSpec(memory_space=pltpu.VMEM),
        scratch_shapes=[
            pltpu.VMEM((STEPS, np_) + tile, f32),
            pltpu.VMEM((STEPS, 4, CAP) + tile, f32),
            pltpu.VMEM((STEPS, 4 * CAP) + tile, f32),
            pltpu.VMEM((STEPS, 4, CAP) + tile, f32),
            pltpu.VMEM((STEPS, bc, rows + 2, 8, values), f32),
            pltpu.VMEM((STEPS, 2, bc, 8, values), f32),
            pltpu.VMEM((STEPS, 2, rows, values), f32),
            pltpu.VMEM((STEPS, 2, rows, values), f32),
            pltpu.VMEM((2, 1, values), f32),
            pltpu.VMEM((2, 1, values), f32),
            pltpu.VMEM((STEPS, 2, values), f32),
            pltpu.VMEM((STEPS, peers, 2, values), f32),
            pltpu.VMEM(source_patch.shape, jnp.int32),
            pltpu.VMEM(shifts.shape, f32),
            pltpu.VMEM((STEPS * source_patch.shape[1], 128), f32),
            pltpu.VMEM((STEPS * 3 * source_patch.shape[1], 128), f32),
            pltpu.VMEM((STEPS * 4 * CAP + 8, 128), jnp.int32),
            pltpu.VMEM((40, 128), f32),
            pltpu.SMEM((STEPS * 4 * CAP + 8, 128), jnp.int32),
            pltpu.SMEM((40, 128), f32),
            pltpu.SMEM((rows,), f32),
            pltpu.SMEM((rows,), f32),
            dma((bc,)),
            dma((5,)),
            dma((STEPS, 4, PIECES)),
            dma((STEPS, 4, PIECES)),
            dma((STEPS, 4)),
            dma((STEPS, 4)),
            dma((2,)),
            dma((2,)),
            dma((STEPS,)),
            dma((STEPS,)),
        ],
        compiler_params=pltpu.CompilerParams(
            collective_id=0, has_side_effects=True, vmem_limit_bytes=32 * 1024 * 1024
        ),
    )(
        *(
            pltpu.with_memory_space_constraint(x, pltpu.HBM)
            for x in (
                source_patch,
                shifts,
                diffusivity,
                tracers.reshape(br, 8, bc, 8, values),
            )
        )
    )
    return result.reshape(rows, cols, values)


def solution(mesh):
    return jax.shard_map(
        functools.partial(local, mesh.shape["lat"], mesh.shape["lon"]),
        mesh=mesh,
        in_specs=(
            P(("groups", "lat"), "lon", None),
            P("groups", None, None, None),
            P("lat"),
            P("groups", None, None),
        ),
        out_specs=P(("groups", "lat"), "lon", None),
        check_vma=False,
    )
```

```python
import functools
import math

import jax
import jax.numpy as jnp
from jax import lax
from jax.experimental import pallas as pl
from jax.experimental.pallas import tpu as pltpu
from jax.sharding import PartitionSpec as P

LEV = 4
STEPS = 2
CAP = 4
OFFSETS = (-2, -1, 1, 2)
SENT_FIRST = (0, 3, 1, 2)
PIECES = 1
PIECE = CAP // PIECES
MESH = pl.DeviceIdType.MESH


def cubic_weights(s):
    return (
        -s * (s - 1.0) * (s - 2.0) * (1.0 / 6.0),
        (s + 1.0) * (s - 1.0) * (s - 2.0) * 0.5,
        -(s + 1.0) * s * (s - 2.0) * 0.5,
        (s + 1.0) * s * (s - 1.0) * (1.0 / 6.0),
    )


def place_weights(w, place, last):
    a, b, c, d = w
    return (
        jnp.where(place == 0, 0.0, a),
        b + jnp.where(place == 0, a, 0.0) + jnp.where(place == last, c + d, 0.0),
        jnp.where(place == last, 0.0, c + jnp.where(place == last - 1, d, 0.0)),
        jnp.where(place >= last - 1, 0.0, d),
    )


def interpolate(rows, weights, ratio):
    values = rows[0].shape[1]
    step = values // LEV
    column = lax.broadcasted_iota(jnp.int32, (8, values), 0)
    level = quotient(lax.broadcasted_iota(jnp.int32, (8, values), 1), step)
    wy, wx, wz = (
        [jnp.full((8, values), w, jnp.float32) for w in part] for part in weights
    )
    a, b, c, d = wy
    ab, cd = a + b, c + d
    bcd = b + cd
    x = rows
    if ratio is not None:
        x = [r * ratio for r in x]
    out = [ab * x[0] + c * x[1] + d * x[2]]
    for i in range(1, 6):
        out.append(a * x[i - 1] + b * x[i] + c * x[i + 1] + d * x[i + 2])
    out.append(a * x[5] + b * x[6] + cd * x[7])
    out.append(a * x[6] + bcd * x[7])
    wx = place_weights(wx, column, 7)
    wz = place_weights(wz, level, LEV - 1)
    done = []
    for v in out:
        v = (
            wx[0] * pltpu.roll(v, 1, 0)
            + wx[1] * v
            + wx[2] * pltpu.roll(v, 7, 0)
            + wx[3] * pltpu.roll(v, 6, 0)
        )
        v = (
            wz[0] * pltpu.roll(v, step, 1)
            + wz[1] * v
            + wz[2] * pltpu.roll(v, values - step, 1)
            + wz[3] * pltpu.roll(v, values - 2 * step, 1)
        )
        done.append(v)
    return done


def quotient(x, n):
    if n & (n - 1) == 0:
        return lax.shift_right_logical(x, jnp.full_like(x, n.bit_length() - 1))
    return lax.div(x, jnp.full_like(x, n))


def make_tables(br, bc, lats, lat, lon, source, shift, near, near_shift, ti, tf):
    np_ = br * bc
    rows = br * 8
    lat_rows, total_cols = source.shape[1:]
    lanes = ti.shape[1]
    lane = lax.broadcasted_iota(jnp.int32, (8, lanes), 1)
    sub = lax.broadcasted_iota(jnp.int32, (8, lanes), 0)
    at = lax.broadcasted_iota(jnp.int32, (total_cols, lanes), 0)
    entry = lax.broadcasted_iota(jnp.int32, (total_cols, lanes), 1)
    pick_columns = jnp.where(at == lon * bc + entry - quotient(entry, bc) * bc, 1.0, 0.0)
    near[...] = jnp.dot(
        source[...].reshape(STEPS * lat_rows, total_cols).astype(jnp.float32),
        pick_columns,
        precision=lax.Precision.HIGHEST,
        preferred_element_type=jnp.float32,
    )
    near_shift[...] = jnp.dot(
        shift[...].reshape(STEPS * 3 * lat_rows, total_cols),
        pick_columns,
        precision=lax.Precision.HIGHEST,
        preferred_element_type=jnp.float32,
    )
    row_of = quotient(lax.broadcasted_iota(jnp.int32, (br, lanes), 1), bc)
    own_row = row_of == lax.broadcasted_iota(jnp.int32, (br, lanes), 0)

    def band(ref, first):
        block = ref[pl.ds(first, br), :]
        return jnp.sum(jnp.where(own_row, block, 0.0), axis=0, keepdims=True)

    parts = [band(near_shift, k * lat_rows + lat * br) for k in range(STEPS * 3)]
    parts += [parts[0]] * (8 - STEPS * 3)
    for k, w in enumerate(cubic_weights(jnp.concatenate(parts, axis=0))):
        tf[8 * k : 8 * k + 8, :] = w
    latitude = ((lat * rows + lane).astype(jnp.float32) + 0.5) * (
        math.pi / (rows * lats)
    ) - 0.5 * math.pi
    tf[32:40, :] = jnp.cos(latitude)

    valid = lane < np_
    dest = jnp.clip(lat + jnp.minimum(sub, 4) - 2, 0, lats - 1)
    own_rows = []
    for s in range(STEPS):
        places = [
            s * lat_rows + jnp.clip(lat + o, 0, lats - 1) * br for o in range(-2, 3)
        ]
        bands = [band(near, p) for p in places]
        bands += [bands[4]] * 3
        ids = jnp.concatenate(bands, axis=0).astype(jnp.int32)
        source_row = quotient(ids, total_cols)
        source_dev = quotient(source_row, br)
        source_q = (ids - source_row * total_cols - lon * bc) * br + (
            source_row - source_dev * br
        )
        relative = source_dev - dest + 2
        count = jnp.zeros((8, lanes), jnp.int32)
        for k in range(5):
            count = jnp.where((relative == k) & valid, 1 << (6 * k), count)
        reach = 1
        while reach < np_:
            count = count + jnp.where(lane >= reach, pltpu.roll(count, reach, 1), 0)
            reach *= 2
        rank = jnp.zeros((8, lanes), jnp.int32)
        for k in range(5):
            field = lax.shift_right_logical(count, jnp.full_like(count, 6 * k))
            rank = jnp.where(relative == k, (field & 63) - 1, rank)
        code = jnp.where((source_dev == lat) & valid, rank, -1)

        def spread(x, picks):
            return jnp.concatenate(
                [jnp.broadcast_to(x[p : p + 1], (CAP, lanes)) for p in picks], axis=0
            )

        outer = (0, 1, 3, 4)
        slot = lax.broadcasted_iota(jnp.int32, (4 * CAP, lanes), 0)
        which = quotient(slot, CAP)
        slot = slot - which * CAP
        which = jnp.where(which >= 2, which + 1, which)
        place = lax.broadcasted_iota(jnp.int32, (4 * CAP, lanes), 1)
        sent = jnp.where(spread(code, outer) == slot, spread(source_q, outer), 0)
        mine = (2,) * 4
        hit = (spread(relative, mine) == which) & (spread(rank, mine) == slot)
        come = jnp.where(hit & (place < np_), place, 0)
        sent = jnp.sum(sent.astype(jnp.float32), axis=1, keepdims=True)
        if s == 0:
            first_sent = jnp.clip(sent.astype(jnp.int32), 0, np_ - 1)
        come = jnp.sum(come.astype(jnp.float32), axis=1, keepdims=True)
        ti[s * 4 * CAP : (s + 1) * 4 * CAP, :] = jnp.clip(
            jnp.where(place == 0, sent, come).astype(jnp.int32), 0, np_ - 1
        )
        here = relative == 2
        outer_place = jnp.where(relative > 2, relative - 1, relative) * CAP + rank
        own_rows.append(jnp.clip(jnp.where(here & valid, source_q, 0), 0, np_ - 1)[2:3])
        outer_place = jnp.clip(outer_place, 0, 4 * CAP - 1)
        own_rows.append(jnp.where(here | ~valid, -1, outer_place)[2:3])
    own_rows += own_rows[:1] * (8 - len(own_rows))
    ti[STEPS * 4 * CAP :, :] = jnp.concatenate(own_rows, axis=0)
    return first_sent


def each_band(br, body, carry):
    return lax.fori_loop(0, br, body, carry)


def wrapped(x, n):
    return jnp.where(x >= n, x - n, x)


def kernel(
    br, bc, lats, lons,
    source_hbm, shift_hbm, kappa_hbm, tr, out,
    st, arr, ia, snd, adv, row_in, side_out, side_in, ka_out, ka_in, mass_out, mass_in,
    source, shift, near, near_shift, ti_v, tf_v, ti, tf, kappa, weight,
    load_sem, small_sem, psend, precv, hsend, hrecv, ksend, krecv, msend, mrecv,
):
    np_ = br * bc
    rows = br * 8
    peers = lats * lons
    values = tr.shape[-1]
    lat = lax.axis_index("lat")
    lon = lax.axis_index("lon")

    small = [
        pltpu.make_async_copy(source_hbm, source, small_sem.at[0]),
        pltpu.make_async_copy(shift_hbm, shift, small_sem.at[1]),
        pltpu.make_async_copy(kappa_hbm, kappa, small_sem.at[2]),
    ]
    for copy in small:
        copy.start()
    loads = [
        pltpu.make_async_copy(
            tr.at[:, :, c], st.at[0, pl.ds(c * br, br)], load_sem.at[c]
        )
        for c in range(bc)
    ]
    for copy in loads:
        copy.start()

    zero = jnp.zeros((8, values), jnp.float32)
    for s in range(STEPS):
        for c in range(bc):
            adv[s, c, 0] = zero
            adv[s, c, rows + 1] = zero
    ka_in[...] = jnp.zeros_like(ka_in)
    row_in[...] = jnp.zeros_like(row_in)

    def peer(k):
        return {"lat": wrapped(lat + k // lons, lats), "lon": wrapped(lon + k % lons, lons)}

    barrier = pltpu.get_barrier_semaphore()

    for k in range(1, peers):
        pl.semaphore_signal(barrier, inc=1, device_id=peer(k), device_id_type=MESH)
    for copy in small:
        copy.wait()
    first_sent = make_tables(
        br, bc, lats, lat, lon, source, shift, near, near_shift, ti_v, tf_v
    )
    to_scalar = [
        pltpu.make_async_copy(ti_v, ti, small_sem.at[3]),
        pltpu.make_async_copy(tf_v, tf, small_sem.at[4]),
    ]
    for copy in to_scalar:
        copy.start()
    pl.semaphore_wait(barrier, peers - 1)

    def in_range(offset):
        return (lat + offset >= 0) & (lat + offset < lats)

    def patch_copy(s, o, h):
        return pltpu.make_async_remote_copy(
            src_ref=snd.at[s, o, pl.ds(h * PIECE, PIECE)],
            dst_ref=arr.at[s, 3 - o, pl.ds(h * PIECE, PIECE)],
            send_sem=psend.at[s, o, h],
            recv_sem=precv.at[s, 3 - o, h],
            device_id={"lat": jnp.clip(lat + OFFSETS[o], 0, lats - 1), "lon": lon},
            device_id_type=MESH,
        )

    def ka_copy(i):
        return pltpu.make_async_remote_copy(
            src_ref=ka_out.at[i],
            dst_ref=ka_in.at[1 - i],
            send_sem=ksend.at[i],
            recv_sem=krecv.at[1 - i],
            device_id={"lat": jnp.clip(lat + 2 * i - 1, 0, lats - 1), "lon": lon},
            device_id_type=MESH,
        )

    def row_copy(s, i):
        return pltpu.make_async_remote_copy(
            src_ref=adv.at[s, :, rows if i else 1],
            dst_ref=row_in.at[s, 1 - i],
            send_sem=hsend.at[s, i],
            recv_sem=hrecv.at[s, 1 - i],
            device_id={"lat": jnp.clip(lat + 2 * i - 1, 0, lats - 1), "lon": lon},
            device_id_type=MESH,
        )

    def column_copy(s, i):
        return pltpu.make_async_remote_copy(
            src_ref=side_out.at[s, i],
            dst_ref=side_in.at[s, 1 - i],
            send_sem=hsend.at[s, 2 + i],
            recv_sem=hrecv.at[s, 3 - i],
            device_id={"lat": lat, "lon": wrapped(lon + (1 if i else lons - 1), lons)},
            device_id_type=MESH,
        )

    def send_patches(s, index):
        for o in SENT_FIRST:
            for h in range(PIECES):
                for j in range(h * PIECE, (h + 1) * PIECE):
                    snd[s, o, j] = st[s, index[o * CAP + j]]

                @pl.when(in_range(OFFSETS[o]))
                def _():
                    patch_copy(s, o, h).start()

    def weights(s, e):
        return [[tf[8 * k + s * 3 + i, e] for k in range(4)] for i in range(3)]

    def masses(s):
        for k in range(1, peers):
            pltpu.make_async_remote_copy(
                src_ref=mass_out.at[s],
                dst_ref=mass_in.at[s, k],
                send_sem=msend.at[s],
                recv_sem=mrecv.at[s],
                device_id=peer(k),
                device_id_type=MESH,
            ).start()

    def masses_sum(s):
        others = mass_in.at[s, pl.ds(1, peers - 1)]
        pltpu.make_async_copy(others, others, mrecv.at[s]).wait()
        return jnp.sum(mass_in[s], axis=0)

    def advect(s, ratio):
        def own(r, _):
            for c in range(bc):
                e = r * bc + c
                block = st[s, ti[STEPS * 4 * CAP + 2 * s, e]]
                done = interpolate([block[i] for i in range(8)], weights(s, e), ratio)
                for i in range(8):
                    adv[s, c, 1 + r * 8 + i] = done[i]
            return 0

        each_band(br, own, 0)
        odd = lat & 1

        def come(o, j):
            e = ti[(s * 4 + o) * CAP + j, 1]
            block = arr[s, o, j]
            done = interpolate([block[i] for i in range(8)], weights(s, e), ratio)
            for i in range(8):
                ia[s, o * CAP + j, i] = done[i]

        def arrived(o):
            offset = o - 2 + jnp.where(o >= 2, 1, 0)

            @pl.when(in_range(offset))
            def _():
                piece = arr.at[s, o]
                pltpu.make_async_copy(piece, piece, precv.at[s, o, 0]).wait()

        arrived(2 - odd)
        for j in range(CAP):
            come(2 - odd, j)
        far = (0, 3, 1 + odd)
        for o in far:
            arrived(o)
        for o in far:
            for j in range(CAP):
                come(o, j)

        def join(r, total):
            sums = [zero] * 8
            for c in range(bc):
                pick = ti[STEPS * 4 * CAP + 2 * s + 1, r * bc + c]
                block = ia[s, jnp.maximum(pick, 0)]
                far = jnp.full((8, values), pick, jnp.int32) >= 0
                for i in range(8):
                    v = jnp.where(far, block[i], adv[s, c, 1 + r * 8 + i])
                    adv[s, c, 1 + r * 8 + i] = v
                    sums[i] = sums[i] + v
            for i in range(8):
                total = total + weight[r * 8 + i] * sums[i]
            return total

        total = each_band(br, join, zero)
        for i in range(2):

            @pl.when(in_range(2 * i - 1))
            def _():
                row_copy(s, i).start()

        for i in range(rows):
            side_out[s, 0, i : i + 1] = adv[s, 0, 1 + i][0:1]
            side_out[s, 1, i : i + 1] = adv[s, bc - 1, 1 + i][7:8]
        for i in range(2):
            column_copy(s, i).start()
        first = functools.reduce(jnp.add, [adv[s, c, 1] for c in range(bc)])
        last = functools.reduce(jnp.add, [adv[s, c, rows] for c in range(bc)])
        return total + first * ka_in[0] + last * ka_in[1]

    def wait_halos(s):
        for i in range(2):

            @pl.when(in_range(2 * i - 1))
            def _():
                row_copy(s, 1 - i).wait_recv()

            column_copy(s, 1 - i).wait_recv()

    column = lax.broadcasted_iota(jnp.int32, (8, values), 0)

    def add_halos(s, place):
        ref, where = place
        for i, row in enumerate((0, rows - 1)):
            for c in range(bc):
                at = where(row // 8, row % 8, c)
                ref[at] = ref[at] + kappa[row] * row_in[s, i, c]

        def sides(r, _):
            for a in range(8):
                row = r * 8 + a
                for i, c in enumerate((0, bc - 1)):
                    at = where(r, a, c)
                    side = jnp.broadcast_to(side_in[s, i, pl.ds(row, 1)], (8, values))
                    side = jnp.where(column == (7 if i else 0), side, 0.0)
                    ref[at] = ref[at] + kappa[row] * side
            return 0

        each_band(br, sides, 0)

    def diffused_row(s, row):
        here = [adv[s, c, 1 + row] for c in range(bc)]
        ahead = [pltpu.roll(v, 7, 0) for v in here]
        behind = [pltpu.roll(v, 1, 0) for v in here]
        number = kappa[row]
        result = []
        for c in range(bc):
            e = jnp.where(column == 7, 0.0 if c == bc - 1 else ahead[c + 1], ahead[c])
            w = jnp.where(column == 0, 0.0 if c == 0 else behind[c - 1], behind[c])
            lap = adv[s, c, row] + adv[s, c, row + 2] + e + w - 4.0 * here[c]
            result.append(here[c] + number * lap)
        return result

    for copy in loads:
        copy.wait()
    send_patches(0, [first_sent[k, 0] for k in range(4 * CAP)])
    for copy in to_scalar:
        copy.wait()

    def area(row):
        return tf[32, row]

    for i, row in enumerate((0, rows - 1)):
        ka_out[i] = jnp.full((1, values), kappa[row] * area(row), jnp.float32)
    for i in range(2):

        @pl.when(in_range(2 * i - 1))
        def _():
            ka_copy(i).start()


    for row in range(rows):
        w = area(row) * (1.0 - 2.0 * kappa[row])
        if row:
            w = w + area(row - 1) * kappa[row - 1]
        if row < rows - 1:
            w = w + area(row + 1) * kappa[row + 1]
        weight[row] = w

    def target_band(r, total):
        for a in range(8):
            parts = [st[0, c * br + r, a] for c in range(bc)]
            total = total + area(r * 8 + a) * functools.reduce(jnp.add, parts)
        return total

    target_part = each_band(br, target_band, zero)
    for i in range(2):

        @pl.when(in_range(2 * i - 1))
        def _():
            ka_copy(1 - i).wait_recv()

    total = advect(0, None)
    both = jnp.concatenate(
        [
            jnp.sum(total, axis=0, keepdims=True),
            jnp.sum(target_part, axis=0, keepdims=True),
        ],
        axis=0,
    )
    mass_out[0] = both
    mass_in[0, 0] = both
    masses(0)

    def in_state(r, a, c):
        return 1, c * br + r, a

    def first_step(r, _):
        for a in range(8):
            done = diffused_row(0, r * 8 + a)
            for c in range(bc):
                st[in_state(r, a, c)] = done[c]
        return 0

    each_band(br, first_step, 0)
    wait_halos(0)
    add_halos(0, (st, in_state))
    send_patches(1, [ti[4 * CAP + k, 0] for k in range(4 * CAP)])
    sums = masses_sum(0)
    target = sums[1:2]
    ratio = jnp.broadcast_to(target / sums[0:1], (8, values))
    total = advect(1, ratio)
    both = jnp.broadcast_to(jnp.sum(total, axis=0, keepdims=True), (2, values))
    mass_out[1] = both
    mass_in[1, 0] = both
    masses(1)

    def in_out(r, a, c):
        return r, a, c

    def last_step(r, _):
        for a in range(8):
            done = diffused_row(1, r * 8 + a)
            for c in range(bc):
                out[in_out(r, a, c)] = done[c]
        return 0

    each_band(br, last_step, 0)
    wait_halos(1)
    add_halos(1, (out, in_out))
    ratio = jnp.broadcast_to(target / masses_sum(1)[0:1], (8, values))

    def scale(r, _):
        for a in range(8):
            for c in range(bc):
                out[r, a, c] = out[r, a, c] * ratio
        return 0

    each_band(br, scale, 0)

    for s in range(STEPS):
        for o in range(4):

            @pl.when(in_range(OFFSETS[o]))
            def _():
                for h in range(PIECES):
                    patch_copy(s, o, h).wait_send()

        for i in range(2):

            @pl.when(in_range(2 * i - 1))
            def _():
                row_copy(s, i).wait_send()

            column_copy(s, i).wait_send()
        others = mass_in.at[s, pl.ds(1, peers - 1)]
        pltpu.make_async_copy(others, others, msend.at[s]).wait()
    for i in range(2):

        @pl.when(in_range(2 * i - 1))
        def _():
            ka_copy(i).wait_send()


def local(lats, lons, tracers, shifts, diffusivity, source_patch):
    rows, cols, values = tracers.shape
    br, bc = rows // 8, cols // 8
    np_ = br * bc
    tile = (8, 8, values)
    peers = lats * lons
    dma = pltpu.SemaphoreType.DMA
    f32 = jnp.float32
    result = pl.pallas_call(
        functools.partial(kernel, br, bc, lats, lons),
        out_shape=pltpu.VMEM((br, 8, bc, 8, values), f32),
        in_specs=[
            pl.BlockSpec(memory_space=pltpu.HBM),
            pl.BlockSpec(memory_space=pltpu.HBM),
            pl.BlockSpec(memory_space=pltpu.HBM),
            pl.BlockSpec(memory_space=pltpu.HBM),
        ],
        out_specs=pl.BlockSpec(memory_space=pltpu.VMEM),
        scratch_shapes=[
            pltpu.VMEM((STEPS, np_) + tile, f32),
            pltpu.VMEM((STEPS, 4, CAP) + tile, f32),
            pltpu.VMEM((STEPS, 4 * CAP) + tile, f32),
            pltpu.VMEM((STEPS, 4, CAP) + tile, f32),
            pltpu.VMEM((STEPS, bc, rows + 2, 8, values), f32),
            pltpu.VMEM((STEPS, 2, bc, 8, values), f32),
            pltpu.VMEM((STEPS, 2, rows, values), f32),
            pltpu.VMEM((STEPS, 2, rows, values), f32),
            pltpu.VMEM((2, 1, values), f32),
            pltpu.VMEM((2, 1, values), f32),
            pltpu.VMEM((STEPS, 2, values), f32),
            pltpu.VMEM((STEPS, peers, 2, values), f32),
            pltpu.VMEM(source_patch.shape, jnp.int32),
            pltpu.VMEM(shifts.shape, f32),
            pltpu.VMEM((STEPS * source_patch.shape[1], 128), f32),
            pltpu.VMEM((STEPS * 3 * source_patch.shape[1], 128), f32),
            pltpu.VMEM((STEPS * 4 * CAP + 8, 128), jnp.int32),
            pltpu.VMEM((40, 128), f32),
            pltpu.SMEM((STEPS * 4 * CAP + 8, 128), jnp.int32),
            pltpu.SMEM((40, 128), f32),
            pltpu.SMEM((rows,), f32),
            pltpu.SMEM((rows,), f32),
            dma((bc,)),
            dma((5,)),
            dma((STEPS, 4, PIECES)),
            dma((STEPS, 4, PIECES)),
            dma((STEPS, 4)),
            dma((STEPS, 4)),
            dma((2,)),
            dma((2,)),
            dma((STEPS,)),
            dma((STEPS,)),
        ],
        compiler_params=pltpu.CompilerParams(
            collective_id=0, has_side_effects=True, vmem_limit_bytes=32 * 1024 * 1024
        ),
    )(
        *(
            pltpu.with_memory_space_constraint(x, pltpu.HBM)
            for x in (
                source_patch,
                shifts,
                diffusivity,
                tracers.reshape(br, 8, bc, 8, values),
            )
        )
    )
    return result.reshape(rows, cols, values)


def solution(mesh):
    return jax.shard_map(
        functools.partial(local, mesh.shape["lat"], mesh.shape["lon"]),
        mesh=mesh,
        in_specs=(
            P(("groups", "lat"), "lon", None),
            P("groups", None, None, None),
            P("lat"),
            P("groups", None, None),
        ),
        out_specs=P(("groups", "lat"), "lon", None),
        check_vma=False,
    )
```

```python
import functools
import math

import jax
import jax.numpy as jnp
from jax import lax
from jax.experimental import pallas as pl
from jax.experimental.pallas import tpu as pltpu
from jax.sharding import PartitionSpec as P

LEV = 4
STEPS = 2
CAP = 4
OFFSETS = (-2, -1, 1, 2)
SENT_FIRST = (0, 3, 1, 2)
PIECES = 2
PIECE = CAP // PIECES
MESH = pl.DeviceIdType.MESH


def cubic_weights(s):
    return (
        -s * (s - 1.0) * (s - 2.0) * (1.0 / 6.0),
        (s + 1.0) * (s - 1.0) * (s - 2.0) * 0.5,
        -(s + 1.0) * s * (s - 2.0) * 0.5,
        (s + 1.0) * s * (s - 1.0) * (1.0 / 6.0),
    )


def place_weights(w, place, last):
    a, b, c, d = w
    return (
        jnp.where(place == 0, 0.0, a),
        b + jnp.where(place == 0, a, 0.0) + jnp.where(place == last, c + d, 0.0),
        jnp.where(place == last, 0.0, c + jnp.where(place == last - 1, d, 0.0)),
        jnp.where(place >= last - 1, 0.0, d),
    )


def interpolate(rows, weights, ratio):
    values = rows[0].shape[1]
    step = values // LEV
    column = lax.broadcasted_iota(jnp.int32, (8, values), 0)
    level = quotient(lax.broadcasted_iota(jnp.int32, (8, values), 1), step)
    wy, wx, wz = (
        [jnp.full((8, values), w, jnp.float32) for w in part] for part in weights
    )
    a, b, c, d = wy
    ab, cd = a + b, c + d
    bcd = b + cd
    x = rows
    if ratio is not None:
        x = [r * ratio for r in x]
    out = [ab * x[0] + c * x[1] + d * x[2]]
    for i in range(1, 6):
        out.append(a * x[i - 1] + b * x[i] + c * x[i + 1] + d * x[i + 2])
    out.append(a * x[5] + b * x[6] + cd * x[7])
    out.append(a * x[6] + bcd * x[7])
    wx = place_weights(wx, column, 7)
    wz = place_weights(wz, level, LEV - 1)
    done = []
    for v in out:
        v = (
            wx[0] * pltpu.roll(v, 1, 0)
            + wx[1] * v
            + wx[2] * pltpu.roll(v, 7, 0)
            + wx[3] * pltpu.roll(v, 6, 0)
        )
        v = (
            wz[0] * pltpu.roll(v, step, 1)
            + wz[1] * v
            + wz[2] * pltpu.roll(v, values - step, 1)
            + wz[3] * pltpu.roll(v, values - 2 * step, 1)
        )
        done.append(v)
    return done


def quotient(x, n):
    if n & (n - 1) == 0:
        return lax.shift_right_logical(x, jnp.full_like(x, n.bit_length() - 1))
    return lax.div(x, jnp.full_like(x, n))


def make_tables(br, bc, lats, lat, lon, source, shift, near, near_shift, ti, tf):
    np_ = br * bc
    rows = br * 8
    lat_rows, total_cols = source.shape[1:]
    lanes = ti.shape[1]
    lane = lax.broadcasted_iota(jnp.int32, (8, lanes), 1)
    sub = lax.broadcasted_iota(jnp.int32, (8, lanes), 0)
    at = lax.broadcasted_iota(jnp.int32, (total_cols, lanes), 0)
    entry = lax.broadcasted_iota(jnp.int32, (total_cols, lanes), 1)
    pick_columns = jnp.where(at == lon * bc + entry - quotient(entry, bc) * bc, 1.0, 0.0)
    near[...] = jnp.dot(
        source[...].reshape(STEPS * lat_rows, total_cols).astype(jnp.float32),
        pick_columns,
        precision=lax.Precision.HIGHEST,
        preferred_element_type=jnp.float32,
    )
    near_shift[...] = jnp.dot(
        shift[...].reshape(STEPS * 3 * lat_rows, total_cols),
        pick_columns,
        precision=lax.Precision.HIGHEST,
        preferred_element_type=jnp.float32,
    )
    row_of = quotient(lax.broadcasted_iota(jnp.int32, (br, lanes), 1), bc)
    own_row = row_of == lax.broadcasted_iota(jnp.int32, (br, lanes), 0)

    def band(ref, first):
        block = ref[pl.ds(first, br), :]
        return jnp.sum(jnp.where(own_row, block, 0.0), axis=0, keepdims=True)

    parts = [band(near_shift, k * lat_rows + lat * br) for k in range(STEPS * 3)]
    parts += [parts[0]] * (8 - STEPS * 3)
    for k, w in enumerate(cubic_weights(jnp.concatenate(parts, axis=0))):
        tf[8 * k : 8 * k + 8, :] = w
    latitude = ((lat * rows + lane).astype(jnp.float32) + 0.5) * (
        math.pi / (rows * lats)
    ) - 0.5 * math.pi
    tf[32:40, :] = jnp.cos(latitude)

    valid = lane < np_
    dest = jnp.clip(lat + jnp.minimum(sub, 4) - 2, 0, lats - 1)
    own_rows = []
    for s in range(STEPS):
        places = [
            s * lat_rows + jnp.clip(lat + o, 0, lats - 1) * br for o in range(-2, 3)
        ]
        bands = [band(near, p) for p in places]
        bands += [bands[4]] * 3
        ids = jnp.concatenate(bands, axis=0).astype(jnp.int32)
        source_row = quotient(ids, total_cols)
        source_dev = quotient(source_row, br)
        source_q = (ids - source_row * total_cols - lon * bc) * br + (
            source_row - source_dev * br
        )
        relative = source_dev - dest + 2
        count = jnp.zeros((8, lanes), jnp.int32)
        for k in range(5):
            count = jnp.where((relative == k) & valid, 1 << (6 * k), count)
        reach = 1
        while reach < np_:
            count = count + jnp.where(lane >= reach, pltpu.roll(count, reach, 1), 0)
            reach *= 2
        rank = jnp.zeros((8, lanes), jnp.int32)
        for k in range(5):
            field = lax.shift_right_logical(count, jnp.full_like(count, 6 * k))
            rank = jnp.where(relative == k, (field & 63) - 1, rank)
        code = jnp.where((source_dev == lat) & valid, rank, -1)

        def spread(x, picks):
            return jnp.concatenate(
                [jnp.broadcast_to(x[p : p + 1], (CAP, lanes)) for p in picks], axis=0
            )

        outer = (0, 1, 3, 4)
        slot = lax.broadcasted_iota(jnp.int32, (4 * CAP, lanes), 0)
        which = quotient(slot, CAP)
        slot = slot - which * CAP
        which = jnp.where(which >= 2, which + 1, which)
        place = lax.broadcasted_iota(jnp.int32, (4 * CAP, lanes), 1)
        sent = jnp.where(spread(code, outer) == slot, spread(source_q, outer), 0)
        mine = (2,) * 4
        hit = (spread(relative, mine) == which) & (spread(rank, mine) == slot)
        come = jnp.where(hit & (place < np_), place, 0)
        sent = jnp.sum(sent.astype(jnp.float32), axis=1, keepdims=True)
        if s == 0:
            first_sent = jnp.clip(sent.astype(jnp.int32), 0, np_ - 1)
        come = jnp.sum(come.astype(jnp.float32), axis=1, keepdims=True)
        ti[s * 4 * CAP : (s + 1) * 4 * CAP, :] = jnp.clip(
            jnp.where(place == 0, sent, come).astype(jnp.int32), 0, np_ - 1
        )
        here = relative == 2
        outer_place = jnp.where(relative > 2, relative - 1, relative) * CAP + rank
        own_rows.append(jnp.clip(jnp.where(here & valid, source_q, 0), 0, np_ - 1)[2:3])
        outer_place = jnp.clip(outer_place, 0, 4 * CAP - 1)
        own_rows.append(jnp.where(here | ~valid, -1, outer_place)[2:3])
    own_rows += own_rows[:1] * (8 - len(own_rows))
    ti[STEPS * 4 * CAP :, :] = jnp.concatenate(own_rows, axis=0)
    return first_sent


def each_band(br, body, carry):
    return lax.fori_loop(0, br, body, carry)


def wrapped(x, n):
    return jnp.where(x >= n, x - n, x)


def kernel(
    br, bc, lats, lons,
    source_hbm, shift_hbm, kappa_hbm, tr, out,
    st, arr, ia, snd, adv, row_in, side_out, side_in, ka_out, ka_in, mass_out, mass_in,
    source, shift, near, near_shift, ti_v, tf_v, ti, tf, kappa, weight,
    load_sem, small_sem, psend, precv, hsend, hrecv, ksend, krecv, msend, mrecv,
):
    np_ = br * bc
    rows = br * 8
    peers = lats * lons
    values = tr.shape[-1]
    lat = lax.axis_index("lat")
    lon = lax.axis_index("lon")

    small = [
        pltpu.make_async_copy(source_hbm, source, small_sem.at[0]),
        pltpu.make_async_copy(shift_hbm, shift, small_sem.at[1]),
        pltpu.make_async_copy(kappa_hbm, kappa, small_sem.at[2]),
    ]
    for copy in small:
        copy.start()
    loads = [
        pltpu.make_async_copy(
            tr.at[:, :, c], st.at[0, pl.ds(c * br, br)], load_sem.at[c]
        )
        for c in range(bc)
    ]
    for copy in loads:
        copy.start()

    zero = jnp.zeros((8, values), jnp.float32)
    for s in range(STEPS):
        for c in range(bc):
            adv[s, c, 0] = zero
            adv[s, c, rows + 1] = zero
    ka_in[...] = jnp.zeros_like(ka_in)
    row_in[...] = jnp.zeros_like(row_in)

    def peer(k):
        return {"lat": wrapped(lat + k // lons, lats), "lon": wrapped(lon + k % lons, lons)}

    barrier = pltpu.get_barrier_semaphore()

    for k in range(1, peers):
        pl.semaphore_signal(barrier, inc=1, device_id=peer(k), device_id_type=MESH)
    for copy in small:
        copy.wait()
    first_sent = make_tables(
        br, bc, lats, lat, lon, source, shift, near, near_shift, ti_v, tf_v
    )
    to_scalar = [
        pltpu.make_async_copy(ti_v, ti, small_sem.at[3]),
        pltpu.make_async_copy(tf_v, tf, small_sem.at[4]),
    ]
    for copy in to_scalar:
        copy.start()
    pl.semaphore_wait(barrier, peers - 1)

    def in_range(offset):
        return (lat + offset >= 0) & (lat + offset < lats)

    def patch_copy(s, o, h):
        return pltpu.make_async_remote_copy(
            src_ref=snd.at[s, o, pl.ds(h * PIECE, PIECE)],
            dst_ref=arr.at[s, 3 - o, pl.ds(h * PIECE, PIECE)],
            send_sem=psend.at[s, o, h],
            recv_sem=precv.at[s, 3 - o, h],
            device_id={"lat": jnp.clip(lat + OFFSETS[o], 0, lats - 1), "lon": lon},
            device_id_type=MESH,
        )

    def ka_copy(i):
        return pltpu.make_async_remote_copy(
            src_ref=ka_out.at[i],
            dst_ref=ka_in.at[1 - i],
            send_sem=ksend.at[i],
            recv_sem=krecv.at[1 - i],
            device_id={"lat": jnp.clip(lat + 2 * i - 1, 0, lats - 1), "lon": lon},
            device_id_type=MESH,
        )

    def row_copy(s, i):
        return pltpu.make_async_remote_copy(
            src_ref=adv.at[s, :, rows if i else 1],
            dst_ref=row_in.at[s, 1 - i],
            send_sem=hsend.at[s, i],
            recv_sem=hrecv.at[s, 1 - i],
            device_id={"lat": jnp.clip(lat + 2 * i - 1, 0, lats - 1), "lon": lon},
            device_id_type=MESH,
        )

    def column_copy(s, i):
        return pltpu.make_async_remote_copy(
            src_ref=side_out.at[s, i],
            dst_ref=side_in.at[s, 1 - i],
            send_sem=hsend.at[s, 2 + i],
            recv_sem=hrecv.at[s, 3 - i],
            device_id={"lat": lat, "lon": wrapped(lon + (1 if i else lons - 1), lons)},
            device_id_type=MESH,
        )

    def send_patches(s, index):
        for o in SENT_FIRST:
            for h in range(PIECES):
                for j in range(h * PIECE, (h + 1) * PIECE):
                    snd[s, o, j] = st[s, index[o * CAP + j]]

                @pl.when(in_range(OFFSETS[o]))
                def _():
                    patch_copy(s, o, h).start()

    def weights(s, e):
        return [[tf[8 * k + s * 3 + i, e] for k in range(4)] for i in range(3)]

    def masses(s):
        for k in range(1, peers):
            pltpu.make_async_remote_copy(
                src_ref=mass_out.at[s],
                dst_ref=mass_in.at[s, k],
                send_sem=msend.at[s],
                recv_sem=mrecv.at[s],
                device_id=peer(k),
                device_id_type=MESH,
            ).start()

    def masses_sum(s):
        others = mass_in.at[s, pl.ds(1, peers - 1)]
        pltpu.make_async_copy(others, others, mrecv.at[s]).wait()
        return jnp.sum(mass_in[s], axis=0)

    def advect(s, ratio):
        def own(r, _):
            for c in range(bc):
                e = r * bc + c
                block = st[s, ti[STEPS * 4 * CAP + 2 * s, e]]
                done = interpolate([block[i] for i in range(8)], weights(s, e), ratio)
                for i in range(8):
                    adv[s, c, 1 + r * 8 + i] = done[i]
            return 0

        each_band(br, own, 0)
        odd = lat & 1

        def come(o, j):
            e = ti[(s * 4 + o) * CAP + j, 1]
            block = arr[s, o, j]
            done = interpolate([block[i] for i in range(8)], weights(s, e), ratio)
            for i in range(8):
                ia[s, o * CAP + j, i] = done[i]

        def arrived(o, halves):
            offset = o - 2 + jnp.where(o >= 2, 1, 0)

            @pl.when(in_range(offset))
            def _():
                for h in range(PIECES):
                    piece = arr.at[s, o, pl.ds(h * PIECE, PIECE)]
                    pltpu.make_async_copy(piece, piece, precv.at[s, o, h]).wait()
                    if halves:
                        for j in range(h * PIECE, (h + 1) * PIECE):
                            come(o, j)
                if not halves:
                    for j in range(CAP):
                        come(o, j)

        arrived(2 - odd, False)
        arrived(0, False)
        arrived(3, False)
        arrived(1 + odd, True)

        def join(r, total):
            sums = [zero] * 8
            for c in range(bc):
                pick = ti[STEPS * 4 * CAP + 2 * s + 1, r * bc + c]
                block = ia[s, jnp.maximum(pick, 0)]
                far = jnp.full((8, values), pick, jnp.int32) >= 0
                for i in range(8):
                    v = jnp.where(far, block[i], adv[s, c, 1 + r * 8 + i])
                    adv[s, c, 1 + r * 8 + i] = v
                    sums[i] = sums[i] + v
            for i in range(8):
                total = total + weight[r * 8 + i] * sums[i]
            return total

        total = each_band(br, join, zero)
        for i in range(2):

            @pl.when(in_range(2 * i - 1))
            def _():
                row_copy(s, i).start()

        for i in range(rows):
            side_out[s, 0, i : i + 1] = adv[s, 0, 1 + i][0:1]
            side_out[s, 1, i : i + 1] = adv[s, bc - 1, 1 + i][7:8]
        for i in range(2):
            column_copy(s, i).start()
        first = functools.reduce(jnp.add, [adv[s, c, 1] for c in range(bc)])
        last = functools.reduce(jnp.add, [adv[s, c, rows] for c in range(bc)])
        return total + first * ka_in[0] + last * ka_in[1]

    def wait_halos(s):
        for i in range(2):

            @pl.when(in_range(2 * i - 1))
            def _():
                row_copy(s, 1 - i).wait_recv()

            column_copy(s, 1 - i).wait_recv()

    column = lax.broadcasted_iota(jnp.int32, (8, values), 0)

    def add_halos(s, place):
        ref, where = place
        for i, row in enumerate((0, rows - 1)):
            for c in range(bc):
                at = where(row // 8, row % 8, c)
                ref[at] = ref[at] + kappa[row] * row_in[s, i, c]

        def sides(r, _):
            for a in range(8):
                row = r * 8 + a
                for i, c in enumerate((0, bc - 1)):
                    at = where(r, a, c)
                    side = jnp.broadcast_to(side_in[s, i, pl.ds(row, 1)], (8, values))
                    side = jnp.where(column == (7 if i else 0), side, 0.0)
                    ref[at] = ref[at] + kappa[row] * side
            return 0

        each_band(br, sides, 0)

    def diffused_row(s, row):
        here = [adv[s, c, 1 + row] for c in range(bc)]
        ahead = [pltpu.roll(v, 7, 0) for v in here]
        behind = [pltpu.roll(v, 1, 0) for v in here]
        number = kappa[row]
        result = []
        for c in range(bc):
            e = jnp.where(column == 7, 0.0 if c == bc - 1 else ahead[c + 1], ahead[c])
            w = jnp.where(column == 0, 0.0 if c == 0 else behind[c - 1], behind[c])
            lap = adv[s, c, row] + adv[s, c, row + 2] + e + w - 4.0 * here[c]
            result.append(here[c] + number * lap)
        return result

    for copy in loads:
        copy.wait()
    send_patches(0, [first_sent[k, 0] for k in range(4 * CAP)])
    for copy in to_scalar:
        copy.wait()

    def area(row):
        return tf[32, row]

    for i, row in enumerate((0, rows - 1)):
        ka_out[i] = jnp.full((1, values), kappa[row] * area(row), jnp.float32)
    for i in range(2):

        @pl.when(in_range(2 * i - 1))
        def _():
            ka_copy(i).start()


    for row in range(rows):
        w = area(row) * (1.0 - 2.0 * kappa[row])
        if row:
            w = w + area(row - 1) * kappa[row - 1]
        if row < rows - 1:
            w = w + area(row + 1) * kappa[row + 1]
        weight[row] = w

    def target_band(r, total):
        for a in range(8):
            parts = [st[0, c * br + r, a] for c in range(bc)]
            total = total + area(r * 8 + a) * functools.reduce(jnp.add, parts)
        return total

    target_part = each_band(br, target_band, zero)
    for i in range(2):

        @pl.when(in_range(2 * i - 1))
        def _():
            ka_copy(1 - i).wait_recv()

    total = advect(0, None)
    both = jnp.concatenate(
        [
            jnp.sum(total, axis=0, keepdims=True),
            jnp.sum(target_part, axis=0, keepdims=True),
        ],
        axis=0,
    )
    mass_out[0] = both
    mass_in[0, 0] = both
    masses(0)

    def in_state(r, a, c):
        return 1, c * br + r, a

    def first_step(r, _):
        for a in range(8):
            done = diffused_row(0, r * 8 + a)
            for c in range(bc):
                st[in_state(r, a, c)] = done[c]
        return 0

    each_band(br, first_step, 0)
    wait_halos(0)
    add_halos(0, (st, in_state))
    send_patches(1, [ti[4 * CAP + k, 0] for k in range(4 * CAP)])
    sums = masses_sum(0)
    target = sums[1:2]
    ratio = jnp.broadcast_to(target / sums[0:1], (8, values))
    total = advect(1, ratio)
    both = jnp.broadcast_to(jnp.sum(total, axis=0, keepdims=True), (2, values))
    mass_out[1] = both
    mass_in[1, 0] = both
    masses(1)

    def in_out(r, a, c):
        return r, a, c

    def last_step(r, _):
        for a in range(8):
            done = diffused_row(1, r * 8 + a)
            for c in range(bc):
                out[in_out(r, a, c)] = done[c]
        return 0

    each_band(br, last_step, 0)
    wait_halos(1)
    add_halos(1, (out, in_out))
    ratio = jnp.broadcast_to(target / masses_sum(1)[0:1], (8, values))

    def scale(r, _):
        for a in range(8):
            for c in range(bc):
                out[r, a, c] = out[r, a, c] * ratio
        return 0

    each_band(br, scale, 0)

    for s in range(STEPS):
        for o in range(4):

            @pl.when(in_range(OFFSETS[o]))
            def _():
                for h in range(PIECES):
                    patch_copy(s, o, h).wait_send()

        for i in range(2):

            @pl.when(in_range(2 * i - 1))
            def _():
                row_copy(s, i).wait_send()

            column_copy(s, i).wait_send()
        others = mass_in.at[s, pl.ds(1, peers - 1)]
        pltpu.make_async_copy(others, others, msend.at[s]).wait()
    for i in range(2):

        @pl.when(in_range(2 * i - 1))
        def _():
            ka_copy(i).wait_send()


def local(lats, lons, tracers, shifts, diffusivity, source_patch):
    rows, cols, values = tracers.shape
    br, bc = rows // 8, cols // 8
    np_ = br * bc
    tile = (8, 8, values)
    peers = lats * lons
    dma = pltpu.SemaphoreType.DMA
    f32 = jnp.float32
    result = pl.pallas_call(
        functools.partial(kernel, br, bc, lats, lons),
        out_shape=pltpu.VMEM((br, 8, bc, 8, values), f32),
        in_specs=[
            pl.BlockSpec(memory_space=pltpu.HBM),
            pl.BlockSpec(memory_space=pltpu.HBM),
            pl.BlockSpec(memory_space=pltpu.HBM),
            pl.BlockSpec(memory_space=pltpu.HBM),
        ],
        out_specs=pl.BlockSpec(memory_space=pltpu.VMEM),
        scratch_shapes=[
            pltpu.VMEM((STEPS, np_) + tile, f32),
            pltpu.VMEM((STEPS, 4, CAP) + tile, f32),
            pltpu.VMEM((STEPS, 4 * CAP) + tile, f32),
            pltpu.VMEM((STEPS, 4, CAP) + tile, f32),
            pltpu.VMEM((STEPS, bc, rows + 2, 8, values), f32),
            pltpu.VMEM((STEPS, 2, bc, 8, values), f32),
            pltpu.VMEM((STEPS, 2, rows, values), f32),
            pltpu.VMEM((STEPS, 2, rows, values), f32),
            pltpu.VMEM((2, 1, values), f32),
            pltpu.VMEM((2, 1, values), f32),
            pltpu.VMEM((STEPS, 2, values), f32),
            pltpu.VMEM((STEPS, peers, 2, values), f32),
            pltpu.VMEM(source_patch.shape, jnp.int32),
            pltpu.VMEM(shifts.shape, f32),
            pltpu.VMEM((STEPS * source_patch.shape[1], 128), f32),
            pltpu.VMEM((STEPS * 3 * source_patch.shape[1], 128), f32),
            pltpu.VMEM((STEPS * 4 * CAP + 8, 128), jnp.int32),
            pltpu.VMEM((40, 128), f32),
            pltpu.SMEM((STEPS * 4 * CAP + 8, 128), jnp.int32),
            pltpu.SMEM((40, 128), f32),
            pltpu.SMEM((rows,), f32),
            pltpu.SMEM((rows,), f32),
            dma((bc,)),
            dma((5,)),
            dma((STEPS, 4, PIECES)),
            dma((STEPS, 4, PIECES)),
            dma((STEPS, 4)),
            dma((STEPS, 4)),
            dma((2,)),
            dma((2,)),
            dma((STEPS,)),
            dma((STEPS,)),
        ],
        compiler_params=pltpu.CompilerParams(
            collective_id=0, has_side_effects=True, vmem_limit_bytes=32 * 1024 * 1024
        ),
    )(
        *(
            pltpu.with_memory_space_constraint(x, pltpu.HBM)
            for x in (
                source_patch,
                shifts,
                diffusivity,
                tracers.reshape(br, 8, bc, 8, values),
            )
        )
    )
    return result.reshape(rows, cols, values)


def solution(mesh):
    return jax.shard_map(
        functools.partial(local, mesh.shape["lat"], mesh.shape["lon"]),
        mesh=mesh,
        in_specs=(
            P(("groups", "lat"), "lon", None),
            P("groups", None, None, None),
            P("lat"),
            P("groups", None, None),
        ),
        out_specs=P(("groups", "lat"), "lon", None),
        check_vma=False,
    )
```

```python
import functools
import math

import jax
import jax.numpy as jnp
from jax import lax
from jax.experimental import pallas as pl
from jax.experimental.pallas import tpu as pltpu
from jax.sharding import PartitionSpec as P

LEV = 4
STEPS = 2
CAP = 4
OFFSETS = (-2, -1, 1, 2)
SENT_FIRST = (0, 3, 1, 2)
PIECES = 2
PIECE = CAP // PIECES
MESH = pl.DeviceIdType.MESH


def cubic_weights(s):
    return (
        -s * (s - 1.0) * (s - 2.0) * (1.0 / 6.0),
        (s + 1.0) * (s - 1.0) * (s - 2.0) * 0.5,
        -(s + 1.0) * s * (s - 2.0) * 0.5,
        (s + 1.0) * s * (s - 1.0) * (1.0 / 6.0),
    )


def place_weights(w, place, last):
    a, b, c, d = w
    return (
        jnp.where(place == 0, 0.0, a),
        b + jnp.where(place == 0, a, 0.0) + jnp.where(place == last, c + d, 0.0),
        jnp.where(place == last, 0.0, c + jnp.where(place == last - 1, d, 0.0)),
        jnp.where(place >= last - 1, 0.0, d),
    )


def interpolate(rows, weights, ratio):
    values = rows[0].shape[1]
    step = values // LEV
    column = lax.broadcasted_iota(jnp.int32, (8, values), 0)
    level = quotient(lax.broadcasted_iota(jnp.int32, (8, values), 1), step)
    wy, wx, wz = (
        [jnp.full((8, values), w, jnp.float32) for w in part] for part in weights
    )
    a, b, c, d = wy
    ab, cd = a + b, c + d
    bcd = b + cd
    x = rows
    if ratio is not None:
        x = [r * ratio for r in x]
    out = [ab * x[0] + c * x[1] + d * x[2]]
    for i in range(1, 6):
        out.append(a * x[i - 1] + b * x[i] + c * x[i + 1] + d * x[i + 2])
    out.append(a * x[5] + b * x[6] + cd * x[7])
    out.append(a * x[6] + bcd * x[7])
    wx = place_weights(wx, column, 7)
    wz = place_weights(wz, level, LEV - 1)
    done = []
    for v in out:
        v = (
            wx[0] * pltpu.roll(v, 1, 0)
            + wx[1] * v
            + wx[2] * pltpu.roll(v, 7, 0)
            + wx[3] * pltpu.roll(v, 6, 0)
        )
        v = (
            wz[0] * pltpu.roll(v, step, 1)
            + wz[1] * v
            + wz[2] * pltpu.roll(v, values - step, 1)
            + wz[3] * pltpu.roll(v, values - 2 * step, 1)
        )
        done.append(v)
    return done


def quotient(x, n):
    if n & (n - 1) == 0:
        return lax.shift_right_logical(x, jnp.full_like(x, n.bit_length() - 1))
    return lax.div(x, jnp.full_like(x, n))


def make_tables(br, bc, lats, lat, lon, source, shift, near, near_shift, ti, tf):
    np_ = br * bc
    rows = br * 8
    lat_rows, total_cols = source.shape[1:]
    lanes = ti.shape[1]
    lane = lax.broadcasted_iota(jnp.int32, (8, lanes), 1)
    sub = lax.broadcasted_iota(jnp.int32, (8, lanes), 0)
    at = lax.broadcasted_iota(jnp.int32, (total_cols, lanes), 0)
    entry = lax.broadcasted_iota(jnp.int32, (total_cols, lanes), 1)
    pick_columns = jnp.where(at == lon * bc + entry - quotient(entry, bc) * bc, 1.0, 0.0)
    near[...] = jnp.dot(
        source[...].reshape(STEPS * lat_rows, total_cols).astype(jnp.float32),
        pick_columns,
        precision=lax.Precision.HIGHEST,
        preferred_element_type=jnp.float32,
    )
    near_shift[...] = jnp.dot(
        shift[...].reshape(STEPS * 3 * lat_rows, total_cols),
        pick_columns,
        precision=lax.Precision.HIGHEST,
        preferred_element_type=jnp.float32,
    )
    row_of = quotient(lax.broadcasted_iota(jnp.int32, (br, lanes), 1), bc)
    own_row = row_of == lax.broadcasted_iota(jnp.int32, (br, lanes), 0)

    def band(ref, first):
        block = ref[pl.ds(first, br), :]
        return jnp.sum(jnp.where(own_row, block, 0.0), axis=0, keepdims=True)

    parts = [band(near_shift, k * lat_rows + lat * br) for k in range(STEPS * 3)]
    parts += [parts[0]] * (8 - STEPS * 3)
    for k, w in enumerate(cubic_weights(jnp.concatenate(parts, axis=0))):
        tf[8 * k : 8 * k + 8, :] = w
    latitude = ((lat * rows + lane).astype(jnp.float32) + 0.5) * (
        math.pi / (rows * lats)
    ) - 0.5 * math.pi
    tf[32:40, :] = jnp.cos(latitude)

    valid = lane < np_
    dest = jnp.clip(lat + jnp.minimum(sub, 4) - 2, 0, lats - 1)
    own_rows = []
    for s in range(STEPS):
        places = [
            s * lat_rows + jnp.clip(lat + o, 0, lats - 1) * br for o in range(-2, 3)
        ]
        bands = [band(near, p) for p in places]
        bands += [bands[4]] * 3
        ids = jnp.concatenate(bands, axis=0).astype(jnp.int32)
        source_row = quotient(ids, total_cols)
        source_dev = quotient(source_row, br)
        source_q = (ids - source_row * total_cols - lon * bc) * br + (
            source_row - source_dev * br
        )
        relative = source_dev - dest + 2
        count = jnp.zeros((8, lanes), jnp.int32)
        for k in range(5):
            count = jnp.where((relative == k) & valid, 1 << (6 * k), count)
        reach = 1
        while reach < np_:
            count = count + jnp.where(lane >= reach, pltpu.roll(count, reach, 1), 0)
            reach *= 2
        rank = jnp.zeros((8, lanes), jnp.int32)
        for k in range(5):
            field = lax.shift_right_logical(count, jnp.full_like(count, 6 * k))
            rank = jnp.where(relative == k, (field & 63) - 1, rank)
        code = jnp.where((source_dev == lat) & valid, rank, -1)

        def spread(x, picks):
            return jnp.concatenate(
                [jnp.broadcast_to(x[p : p + 1], (CAP, lanes)) for p in picks], axis=0
            )

        outer = (0, 1, 3, 4)
        slot = lax.broadcasted_iota(jnp.int32, (4 * CAP, lanes), 0)
        which = quotient(slot, CAP)
        slot = slot - which * CAP
        which = jnp.where(which >= 2, which + 1, which)
        place = lax.broadcasted_iota(jnp.int32, (4 * CAP, lanes), 1)
        sent = jnp.where(spread(code, outer) == slot, spread(source_q, outer), 0)
        mine = (2,) * 4
        hit = (spread(relative, mine) == which) & (spread(rank, mine) == slot)
        come = jnp.where(hit & (place < np_), place, 0)
        sent = jnp.sum(sent.astype(jnp.float32), axis=1, keepdims=True)
        if s == 0:
            first_sent = jnp.clip(sent.astype(jnp.int32), 0, np_ - 1)
        come = jnp.sum(come.astype(jnp.float32), axis=1, keepdims=True)
        ti[s * 4 * CAP : (s + 1) * 4 * CAP, :] = jnp.clip(
            jnp.where(place == 0, sent, come).astype(jnp.int32), 0, np_ - 1
        )
        here = relative == 2
        outer_place = jnp.where(relative > 2, relative - 1, relative) * CAP + rank
        own_rows.append(jnp.clip(jnp.where(here & valid, source_q, 0), 0, np_ - 1)[2:3])
        outer_place = jnp.clip(outer_place, 0, 4 * CAP - 1)
        own_rows.append(jnp.where(here | ~valid, -1, outer_place)[2:3])
    own_rows += own_rows[:1] * (8 - len(own_rows))
    ti[STEPS * 4 * CAP :, :] = jnp.concatenate(own_rows, axis=0)
    return first_sent


def each_band(br, body, carry):
    return lax.fori_loop(0, br, body, carry)


def wrapped(x, n):
    return jnp.where(x >= n, x - n, x)


def kernel(
    br, bc, lats, lons,
    source_hbm, shift_hbm, kappa_hbm, tr, out, ratio_out,
    st, arr, ia, snd, adv, row_in, side_out, side_in, ka_out, ka_in, mass_out, mass_in,
    source, shift, near, near_shift, ti_v, tf_v, ti, tf, kappa, weight,
    load_sem, small_sem, psend, precv, hsend, hrecv, ksend, krecv, msend, mrecv,
):
    np_ = br * bc
    rows = br * 8
    peers = lats * lons
    values = tr.shape[-1]
    lat = lax.axis_index("lat")
    lon = lax.axis_index("lon")

    small = [
        pltpu.make_async_copy(source_hbm, source, small_sem.at[0]),
        pltpu.make_async_copy(shift_hbm, shift, small_sem.at[1]),
        pltpu.make_async_copy(kappa_hbm, kappa, small_sem.at[2]),
    ]
    for copy in small:
        copy.start()
    loads = [
        pltpu.make_async_copy(
            tr.at[:, :, c], st.at[0, pl.ds(c * br, br)], load_sem.at[c]
        )
        for c in range(bc)
    ]
    for copy in loads:
        copy.start()

    zero = jnp.zeros((8, values), jnp.float32)
    for s in range(STEPS):
        for c in range(bc):
            adv[s, c, 0] = zero
            adv[s, c, rows + 1] = zero
    ka_in[...] = jnp.zeros_like(ka_in)
    row_in[...] = jnp.zeros_like(row_in)

    def peer(k):
        return {"lat": wrapped(lat + k // lons, lats), "lon": wrapped(lon + k % lons, lons)}

    barrier = pltpu.get_barrier_semaphore()

    for k in range(1, peers):
        pl.semaphore_signal(barrier, inc=1, device_id=peer(k), device_id_type=MESH)
    for copy in small:
        copy.wait()
    first_sent = make_tables(
        br, bc, lats, lat, lon, source, shift, near, near_shift, ti_v, tf_v
    )
    to_scalar = [
        pltpu.make_async_copy(ti_v, ti, small_sem.at[3]),
        pltpu.make_async_copy(tf_v, tf, small_sem.at[4]),
    ]
    for copy in to_scalar:
        copy.start()
    pl.semaphore_wait(barrier, peers - 1)

    def in_range(offset):
        return (lat + offset >= 0) & (lat + offset < lats)

    def patch_copy(s, o, h):
        return pltpu.make_async_remote_copy(
            src_ref=snd.at[s, o, pl.ds(h * PIECE, PIECE)],
            dst_ref=arr.at[s, 3 - o, pl.ds(h * PIECE, PIECE)],
            send_sem=psend.at[s, o, h],
            recv_sem=precv.at[s, 3 - o, h],
            device_id={"lat": jnp.clip(lat + OFFSETS[o], 0, lats - 1), "lon": lon},
            device_id_type=MESH,
        )

    def ka_copy(i):
        return pltpu.make_async_remote_copy(
            src_ref=ka_out.at[i],
            dst_ref=ka_in.at[1 - i],
            send_sem=ksend.at[i],
            recv_sem=krecv.at[1 - i],
            device_id={"lat": jnp.clip(lat + 2 * i - 1, 0, lats - 1), "lon": lon},
            device_id_type=MESH,
        )

    def row_copy(s, i):
        return pltpu.make_async_remote_copy(
            src_ref=adv.at[s, :, rows if i else 1],
            dst_ref=row_in.at[s, 1 - i],
            send_sem=hsend.at[s, i],
            recv_sem=hrecv.at[s, 1 - i],
            device_id={"lat": jnp.clip(lat + 2 * i - 1, 0, lats - 1), "lon": lon},
            device_id_type=MESH,
        )

    def column_copy(s, i):
        return pltpu.make_async_remote_copy(
            src_ref=side_out.at[s, i],
            dst_ref=side_in.at[s, 1 - i],
            send_sem=hsend.at[s, 2 + i],
            recv_sem=hrecv.at[s, 3 - i],
            device_id={"lat": lat, "lon": wrapped(lon + (1 if i else lons - 1), lons)},
            device_id_type=MESH,
        )

    def send_patches(s, index):
        for o in SENT_FIRST:
            for h in range(PIECES):
                for j in range(h * PIECE, (h + 1) * PIECE):
                    snd[s, o, j] = st[s, index[o * CAP + j]]

                @pl.when(in_range(OFFSETS[o]))
                def _():
                    patch_copy(s, o, h).start()

    def weights(s, e):
        return [[tf[8 * k + s * 3 + i, e] for k in range(4)] for i in range(3)]

    def masses(s):
        for k in range(1, peers):
            pltpu.make_async_remote_copy(
                src_ref=mass_out.at[s],
                dst_ref=mass_in.at[s, k],
                send_sem=msend.at[s],
                recv_sem=mrecv.at[s],
                device_id=peer(k),
                device_id_type=MESH,
            ).start()

    def masses_sum(s):
        others = mass_in.at[s, pl.ds(1, peers - 1)]
        pltpu.make_async_copy(others, others, mrecv.at[s]).wait()
        return jnp.sum(mass_in[s], axis=0)

    def advect(s, ratio):
        def own(r, _):
            for c in range(bc):
                e = r * bc + c
                block = st[s, ti[STEPS * 4 * CAP + 2 * s, e]]
                done = interpolate([block[i] for i in range(8)], weights(s, e), ratio)
                for i in range(8):
                    adv[s, c, 1 + r * 8 + i] = done[i]
            return 0

        each_band(br, own, 0)
        odd = lat & 1

        def come(o, j):
            e = ti[(s * 4 + o) * CAP + j, 1]
            block = arr[s, o, j]
            done = interpolate([block[i] for i in range(8)], weights(s, e), ratio)
            for i in range(8):
                ia[s, o * CAP + j, i] = done[i]

        def arrived(o, halves):
            offset = o - 2 + jnp.where(o >= 2, 1, 0)

            @pl.when(in_range(offset))
            def _():
                for h in range(PIECES):
                    piece = arr.at[s, o, pl.ds(h * PIECE, PIECE)]
                    pltpu.make_async_copy(piece, piece, precv.at[s, o, h]).wait()
                    if halves:
                        for j in range(h * PIECE, (h + 1) * PIECE):
                            come(o, j)
                if not halves:
                    for j in range(CAP):
                        come(o, j)

        arrived(2 - odd, False)
        arrived(0, False)
        arrived(3, False)
        arrived(1 + odd, True)

        def join(r, total):
            sums = [zero] * 8
            for c in range(bc):
                pick = ti[STEPS * 4 * CAP + 2 * s + 1, r * bc + c]
                block = ia[s, jnp.maximum(pick, 0)]
                far = jnp.full((8, values), pick, jnp.int32) >= 0
                for i in range(8):
                    v = jnp.where(far, block[i], adv[s, c, 1 + r * 8 + i])
                    adv[s, c, 1 + r * 8 + i] = v
                    sums[i] = sums[i] + v
            for i in range(8):
                total = total + weight[r * 8 + i] * sums[i]
            return total

        total = each_band(br, join, zero)
        for i in range(2):

            @pl.when(in_range(2 * i - 1))
            def _():
                row_copy(s, i).start()

        for i in range(rows):
            side_out[s, 0, i : i + 1] = adv[s, 0, 1 + i][0:1]
            side_out[s, 1, i : i + 1] = adv[s, bc - 1, 1 + i][7:8]
        for i in range(2):
            column_copy(s, i).start()
        first = functools.reduce(jnp.add, [adv[s, c, 1] for c in range(bc)])
        last = functools.reduce(jnp.add, [adv[s, c, rows] for c in range(bc)])
        return total + first * ka_in[0] + last * ka_in[1]

    def wait_halos(s):
        for i in range(2):

            @pl.when(in_range(2 * i - 1))
            def _():
                row_copy(s, 1 - i).wait_recv()

            column_copy(s, 1 - i).wait_recv()

    column = lax.broadcasted_iota(jnp.int32, (8, values), 0)

    def add_halos(s, place):
        ref, where = place
        for i, row in enumerate((0, rows - 1)):
            for c in range(bc):
                at = where(row // 8, row % 8, c)
                ref[at] = ref[at] + kappa[row] * row_in[s, i, c]

        def sides(r, _):
            for a in range(8):
                row = r * 8 + a
                for i, c in enumerate((0, bc - 1)):
                    at = where(r, a, c)
                    side = jnp.broadcast_to(side_in[s, i, pl.ds(row, 1)], (8, values))
                    side = jnp.where(column == (7 if i else 0), side, 0.0)
                    ref[at] = ref[at] + kappa[row] * side
            return 0

        each_band(br, sides, 0)

    def diffused_row(s, row):
        here = [adv[s, c, 1 + row] for c in range(bc)]
        ahead = [pltpu.roll(v, 7, 0) for v in here]
        behind = [pltpu.roll(v, 1, 0) for v in here]
        number = kappa[row]
        result = []
        for c in range(bc):
            e = jnp.where(column == 7, 0.0 if c == bc - 1 else ahead[c + 1], ahead[c])
            w = jnp.where(column == 0, 0.0 if c == 0 else behind[c - 1], behind[c])
            lap = adv[s, c, row] + adv[s, c, row + 2] + e + w - 4.0 * here[c]
            result.append(here[c] + number * lap)
        return result

    for copy in loads:
        copy.wait()
    send_patches(0, [first_sent[k, 0] for k in range(4 * CAP)])
    for copy in to_scalar:
        copy.wait()

    def area(row):
        return tf[32, row]

    for i, row in enumerate((0, rows - 1)):
        ka_out[i] = jnp.full((1, values), kappa[row] * area(row), jnp.float32)
    for i in range(2):

        @pl.when(in_range(2 * i - 1))
        def _():
            ka_copy(i).start()


    for row in range(rows):
        w = area(row) * (1.0 - 2.0 * kappa[row])
        if row:
            w = w + area(row - 1) * kappa[row - 1]
        if row < rows - 1:
            w = w + area(row + 1) * kappa[row + 1]
        weight[row] = w

    def target_band(r, total):
        for a in range(8):
            parts = [st[0, c * br + r, a] for c in range(bc)]
            total = total + area(r * 8 + a) * functools.reduce(jnp.add, parts)
        return total

    target_part = each_band(br, target_band, zero)
    for i in range(2):

        @pl.when(in_range(2 * i - 1))
        def _():
            ka_copy(1 - i).wait_recv()

    total = advect(0, None)
    both = jnp.concatenate(
        [
            jnp.sum(total, axis=0, keepdims=True),
            jnp.sum(target_part, axis=0, keepdims=True),
        ],
        axis=0,
    )
    mass_out[0] = both
    mass_in[0, 0] = both
    masses(0)

    def in_state(r, a, c):
        return 1, c * br + r, a

    def first_step(r, _):
        for a in range(8):
            done = diffused_row(0, r * 8 + a)
            for c in range(bc):
                st[in_state(r, a, c)] = done[c]
        return 0

    each_band(br, first_step, 0)
    wait_halos(0)
    add_halos(0, (st, in_state))
    send_patches(1, [ti[4 * CAP + k, 0] for k in range(4 * CAP)])
    sums = masses_sum(0)
    target = sums[1:2]
    ratio = jnp.broadcast_to(target / sums[0:1], (8, values))
    total = advect(1, ratio)
    both = jnp.broadcast_to(jnp.sum(total, axis=0, keepdims=True), (2, values))
    mass_out[1] = both
    mass_in[1, 0] = both
    masses(1)

    def in_out(r, a, c):
        return r, a, c

    def last_step(r, _):
        for a in range(8):
            done = diffused_row(1, r * 8 + a)
            for c in range(bc):
                out[in_out(r, a, c)] = done[c]
        return 0

    each_band(br, last_step, 0)
    wait_halos(1)
    add_halos(1, (out, in_out))
    ratio_out[...] = jnp.broadcast_to(target / masses_sum(1)[0:1], (8, values))

    for s in range(STEPS):
        for o in range(4):

            @pl.when(in_range(OFFSETS[o]))
            def _():
                for h in range(PIECES):
                    patch_copy(s, o, h).wait_send()

        for i in range(2):

            @pl.when(in_range(2 * i - 1))
            def _():
                row_copy(s, i).wait_send()

            column_copy(s, i).wait_send()
        others = mass_in.at[s, pl.ds(1, peers - 1)]
        pltpu.make_async_copy(others, others, msend.at[s]).wait()
    for i in range(2):

        @pl.when(in_range(2 * i - 1))
        def _():
            ka_copy(i).wait_send()


def scale_kernel(field, ratio, out, scaled, sems):
    br, _, bc = field.shape[:3]
    factor = ratio[...]
    copies = []
    for r in range(br):
        for h in range(2):
            for a in range(4 * h, 4 * h + 4):
                for c in range(bc):
                    scaled[r, a, c] = field[r, a, c] * factor
            part = pl.ds(4 * h, 4)
            copy = pltpu.make_async_copy(
                scaled.at[r, part], out.at[r, part], sems.at[r, h]
            )
            copy.start()
            copies.append(copy)
    for copy in copies:
        copy.wait()


def local(lats, lons, tracers, shifts, diffusivity, source_patch):
    rows, cols, values = tracers.shape
    br, bc = rows // 8, cols // 8
    np_ = br * bc
    tile = (8, 8, values)
    peers = lats * lons
    dma = pltpu.SemaphoreType.DMA
    f32 = jnp.float32
    field, ratio = pl.pallas_call(
        functools.partial(kernel, br, bc, lats, lons),
        out_shape=(pltpu.VMEM((br, 8, bc, 8, values), f32), pltpu.VMEM((8, values), f32)),
        in_specs=[
            pl.BlockSpec(memory_space=pltpu.HBM),
            pl.BlockSpec(memory_space=pltpu.HBM),
            pl.BlockSpec(memory_space=pltpu.HBM),
            pl.BlockSpec(memory_space=pltpu.HBM),
        ],
        out_specs=(pl.BlockSpec(memory_space=pltpu.VMEM),) * 2,
        scratch_shapes=[
            pltpu.VMEM((STEPS, np_) + tile, f32),
            pltpu.VMEM((STEPS, 4, CAP) + tile, f32),
            pltpu.VMEM((STEPS, 4 * CAP) + tile, f32),
            pltpu.VMEM((STEPS, 4, CAP) + tile, f32),
            pltpu.VMEM((STEPS, bc, rows + 2, 8, values), f32),
            pltpu.VMEM((STEPS, 2, bc, 8, values), f32),
            pltpu.VMEM((STEPS, 2, rows, values), f32),
            pltpu.VMEM((STEPS, 2, rows, values), f32),
            pltpu.VMEM((2, 1, values), f32),
            pltpu.VMEM((2, 1, values), f32),
            pltpu.VMEM((STEPS, 2, values), f32),
            pltpu.VMEM((STEPS, peers, 2, values), f32),
            pltpu.VMEM(source_patch.shape, jnp.int32),
            pltpu.VMEM(shifts.shape, f32),
            pltpu.VMEM((STEPS * source_patch.shape[1], 128), f32),
            pltpu.VMEM((STEPS * 3 * source_patch.shape[1], 128), f32),
            pltpu.VMEM((STEPS * 4 * CAP + 8, 128), jnp.int32),
            pltpu.VMEM((40, 128), f32),
            pltpu.SMEM((STEPS * 4 * CAP + 8, 128), jnp.int32),
            pltpu.SMEM((40, 128), f32),
            pltpu.SMEM((rows,), f32),
            pltpu.SMEM((rows,), f32),
            dma((bc,)),
            dma((5,)),
            dma((STEPS, 4, PIECES)),
            dma((STEPS, 4, PIECES)),
            dma((STEPS, 4)),
            dma((STEPS, 4)),
            dma((2,)),
            dma((2,)),
            dma((STEPS,)),
            dma((STEPS,)),
        ],
        compiler_params=pltpu.CompilerParams(
            collective_id=0, has_side_effects=True, vmem_limit_bytes=32 * 1024 * 1024
        ),
    )(
        *(
            pltpu.with_memory_space_constraint(x, pltpu.HBM)
            for x in (
                source_patch,
                shifts,
                diffusivity,
                tracers.reshape(br, 8, bc, 8, values),
            )
        )
    )
    result = pl.pallas_call(
        scale_kernel,
        out_shape=jax.ShapeDtypeStruct(field.shape, f32),
        in_specs=[pl.BlockSpec(memory_space=pltpu.VMEM)] * 2,
        out_specs=pl.BlockSpec(memory_space=pltpu.HBM),
        scratch_shapes=[pltpu.VMEM(field.shape, f32), dma((br, 2))],
    )(field, ratio)
    return result.reshape(rows, cols, values)


def solution(mesh):
    return jax.shard_map(
        functools.partial(local, mesh.shape["lat"], mesh.shape["lon"]),
        mesh=mesh,
        in_specs=(
            P(("groups", "lat"), "lon", None),
            P("groups", None, None, None),
            P("lat"),
            P("groups", None, None),
        ),
        out_specs=P(("groups", "lat"), "lon", None),
        check_vma=False,
    )
```
